128 devices in a mesh: row: 16 (over z, y), col: 8 (over x, core).
Axes of the slice: x: 4, y: 4, z: 4, core: 2. Of those that a mesh axis runs over, the one named last changes fastest.
Arguments:
- inputs: bfloat16 [256, 16384], P('col', 'row'), may hold values from -6 to 6
- grad_out: bfloat16 [256, 16384], P('col', 'row'), may hold values from -6 to 6
- gate_blocks: bfloat16 [16, 8, 96, 128, 128], P('row', 'col'), may hold values from -0.09375 to 0.09375
- up_blocks: bfloat16 [16, 8, 96, 128, 128], P('row', 'col'), may hold values from -0.09375 to 0.09375
- down_blocks: bfloat16 [16, 8, 96, 128, 128], P('row', 'col'), may hold values from -0.078125 to 0.078125
- gate_slots: int32 [16, 8, 96], P('row', 'col'), may hold values from 0 to 207, as said below
- gate_count: int32 [16, 8], P('row', 'col'), may hold values from 12 to 96, as said below
- down_slots: int32 [16, 8, 96], P('row', 'col'), may hold values from 0 to 207, as said below
- down_count: int32 [16, 8], P('row', 'col'), may hold values from 12 to 96, as said below
Outputs:
- layer_out: bfloat16 [256, 16384], P('col', 'row')
- grad_x: bfloat16 [256, 16384], P('col', 'row')
- grad_gate_blocks: bfloat16 [16, 8, 96, 128, 128], P('row', 'col')
- grad_up_blocks: bfloat16 [16, 8, 96, 128, 128], P('row', 'col')
- grad_down_blocks: bfloat16 [16, 8, 96, 128, 128], P('row', 'col')
The draws below stay inside these ranges and needn't reach their ends.
Inputs may be any that keep to these rules, and one draw needn't show every extreme that they name: `gate_slots`: the 96 entries of one device are distinct positions in its 8 x 26 grid of blocks. `down_slots`: the 96 entries of one device are distinct positions in its 8 x 26 grid of blocks. `gate_count`: some device has all 96 slots live. `down_count`: some device has all 96 slots live.
All inputs are finite; a program needn't handle non-finite values.
Results may differ from the reference program's by a relative error of at most 0.03.
Values may be sent and summed in bfloat16 or wider, within the bound.
A program may use at most 192 MiB of HBM per device.

```python
import jax
import jax.numpy as jnp
from jax import lax

D = 16384
FF = 26624
BLOCK = 128
NB = 96
TOKENS = 256
DPB = 8
FPB = 26
N_ROW = 16
N_COL = 8


def slot_table(key):
    owners = jax.random.split(key, N_ROW * N_COL)
    orders = jax.vmap(lambda owner_key: jax.random.permutation(owner_key, DPB * FPB))(owners)
    return orders[:, :NB].reshape(N_ROW, N_COL, NB).astype(jnp.int32)


def count_table(key):
    lowest = max(1, NB // 8)
    levels = 16
    first_key, second_key = jax.random.split(key)
    picks = jax.random.randint(first_key, (N_ROW * N_COL,), 0, levels)
    counts = lowest + picks * picks * (NB - lowest) // ((levels - 1) * (levels - 1))
    order = jax.random.permutation(second_key, N_ROW * N_COL)
    counts = counts.at[order[0]].set(NB).at[order[1]].set(lowest)
    return counts.reshape(N_ROW, N_COL).astype(jnp.int32)


def draw_gate_slots(key, part):
    key = jax.random.fold_in(key, 11)
    return slot_table(key)


def draw_down_slots(key, part):
    key = jax.random.fold_in(key, 12)
    return slot_table(key)


def draw_gate_count(key, part):
    key = jax.random.fold_in(key, 13)
    return count_table(key)


def draw_down_count(key, part):
    key = jax.random.fold_in(key, 14)
    return count_table(key)


def steps_of(own_key, shape, cuts, least, largest):
    gain = 1.0
    for position, blocks in cuts:
        heights = jax.random.uniform(jax.random.fold_in(jax.random.fold_in(own_key, 6), position), (blocks,), jnp.float32, least / len(cuts), largest / len(cuts))
        gain = gain * jnp.repeat(jnp.exp(heights), shape[position] // blocks).reshape((-1,) + (1,) * (len(shape) - 1 - position))
    return gain


def normal_values(stream_key, dims, scale, most, shards=(), kind=jnp.bfloat16):
    factor_of = steps_of(stream_key, dims, shards, -0.22, 0.18) if shards else 1.0
    array = jax.random.normal(stream_key, dims, jnp.float32) * scale * factor_of
    return jnp.minimum(jnp.maximum(array, -most), most).astype(kind)


def setup_inputs(seed: int = 0) -> dict:
    streams_of = jax.random.split(jax.random.key(seed), 10)
    inputs = normal_values(streams_of[0], (TOKENS, D), 1.0, 6.0, ((0, 8), (1, 16)))
    grad_out = normal_values(streams_of[1], (TOKENS, D), 1.0, 6.0, ((0, 8), (1, 16)))
    gate_blocks = normal_values(streams_of[2], (N_ROW, N_COL, NB, BLOCK, BLOCK), (D // 4) ** -0.5, 0.09375, ((0, 16), (1, 8)))
    up_blocks = normal_values(streams_of[3], (N_ROW, N_COL, NB, BLOCK, BLOCK), (D // 4) ** -0.5, 0.09375, ((0, 16), (1, 8)))
    down_blocks = normal_values(streams_of[4], (N_ROW, N_COL, NB, BLOCK, BLOCK), (FF // 4) ** -0.5, 0.078125, ((0, 16), (1, 8)))
    gate_slots = draw_gate_slots(jax.random.fold_in(streams_of[9], 71), 0)
    gate_count = draw_gate_count(jax.random.fold_in(streams_of[9], 71), 0)
    down_slots = draw_down_slots(jax.random.fold_in(streams_of[9], 71), 0)
    down_count = draw_down_count(jax.random.fold_in(streams_of[9], 71), 0)
    return dict(inputs=inputs, grad_out=grad_out, gate_blocks=gate_blocks, up_blocks=up_blocks, down_blocks=down_blocks, gate_slots=gate_slots, gate_count=gate_count, down_slots=down_slots, down_count=down_count)


def row_grid(blocks, slots, count, row):
    tiles = lax.dynamic_index_in_dim(blocks, row, 0, keepdims=False)
    spots = lax.dynamic_index_in_dim(slots, row, 0, keepdims=False)
    filled = lax.dynamic_index_in_dim(count, row, 0, keepdims=False)
    live = jnp.arange(NB, dtype=jnp.int32)[None, :] < filled[:, None]
    values = jnp.where(live[:, :, None, None], tiles, jnp.zeros_like(tiles))
    column_ids = jnp.arange(N_COL, dtype=jnp.int32)[:, None] * jnp.ones_like(spots)
    grid = jnp.zeros((N_COL, DPB, FPB, BLOCK, BLOCK), tiles.dtype)
    return grid.at[column_ids, spots // FPB, spots % FPB].add(values)


def weight_panels(grid):
    return grid.transpose(0, 1, 3, 2, 4).reshape(N_COL, DPB * BLOCK, FPB * BLOCK).astype(jnp.float32)


def down_panels(grid):
    return grid.transpose(0, 2, 3, 1, 4).reshape(N_COL, FPB * BLOCK, DPB * BLOCK).astype(jnp.float32)


def barrier_round(values):
    rounded = lax.optimization_barrier(values.astype(jnp.bfloat16))
    return rounded.astype(jnp.float32)


def reference(inputs, grad_out, gate_blocks, up_blocks, down_blocks, gate_slots, gate_count, down_slots, down_count):
    d_panel = DPB * BLOCK
    f_panel = FPB * BLOCK
    row_ids = jnp.arange(N_ROW, dtype=jnp.int32)
    zero_field = jnp.zeros((TOKENS, FF), jnp.float32)
    zero_scalar = jnp.zeros((), jnp.float32)

    def forward_step(carry, row):
        gate, up = carry
        x_panel = lax.dynamic_slice_in_dim(inputs, row * d_panel, d_panel, 1).astype(jnp.float32)
        gate_w = weight_panels(row_grid(gate_blocks, gate_slots, gate_count, row))
        up_w = weight_panels(row_grid(up_blocks, gate_slots, gate_count, row))
        gate_term = jnp.einsum("tk,ckf->tcf", x_panel, gate_w).reshape(TOKENS, FF)
        up_term = jnp.einsum("tk,ckf->tcf", x_panel, up_w).reshape(TOKENS, FF)
        return (gate + barrier_round(gate_term), up + barrier_round(up_term)), None

    (gate, up), _ = lax.scan(forward_step, (zero_field, zero_field), row_ids)
    hidden = (jax.nn.silu(gate) * up).astype(jnp.bfloat16)
    hidden_split = hidden.astype(jnp.float32).reshape(TOKENS, N_COL, f_panel)

    def output_step(carry, row):
        down_w = down_panels(row_grid(down_blocks, down_slots, down_count, row))
        terms = jnp.einsum("tcf,cfk->ctk", hidden_split, down_w)
        return carry, jnp.sum(barrier_round(terms), axis=0).astype(jnp.bfloat16)

    _, out_panels = lax.scan(output_step, zero_scalar, row_ids)
    layer_out = out_panels.transpose(1, 0, 2).reshape(TOKENS, D)

    def hidden_grad_step(carry, row):
        cot_panel = lax.dynamic_slice_in_dim(grad_out, row * d_panel, d_panel, 1).astype(jnp.float32)
        down_w = down_panels(row_grid(down_blocks, down_slots, down_count, row))
        terms = jnp.einsum("tk,cfk->tcf", cot_panel, down_w).reshape(TOKENS, FF)
        return carry + barrier_round(terms), None

    grad_hidden, _ = lax.scan(hidden_grad_step, zero_field, row_ids)
    sigma = jax.nn.sigmoid(gate)
    grad_gate = (grad_hidden * up * sigma * (1.0 + gate * (1.0 - sigma))).astype(jnp.bfloat16)
    grad_up = (grad_hidden * gate * sigma).astype(jnp.bfloat16)
    gate_split = grad_gate.astype(jnp.float32).reshape(TOKENS, N_COL, f_panel)
    up_split = grad_up.astype(jnp.float32).reshape(TOKENS, N_COL, f_panel)

    def input_step(carry, row):
        gate_w = weight_panels(row_grid(gate_blocks, gate_slots, gate_count, row))
        up_w = weight_panels(row_grid(up_blocks, gate_slots, gate_count, row))
        terms = jnp.einsum("tcf,ckf->ctk", gate_split, gate_w) + jnp.einsum("tcf,ckf->ctk", up_split, up_w)
        return carry, jnp.sum(barrier_round(terms), axis=0).astype(jnp.bfloat16)

    _, input_panels = lax.scan(input_step, zero_scalar, row_ids)
    grad_x = input_panels.transpose(1, 0, 2).reshape(TOKENS, D)

    gate_grid = gate_split.reshape(TOKENS, N_COL, FPB, BLOCK)
    up_grid = up_split.reshape(TOKENS, N_COL, FPB, BLOCK)
    hid_grid = hidden_split.reshape(TOKENS, N_COL, FPB, BLOCK)

    def block_grads(row):
        x_panel = lax.dynamic_slice_in_dim(inputs, row * d_panel, d_panel, 1).astype(jnp.float32).reshape(TOKENS, DPB, BLOCK)
        cot_panel = lax.dynamic_slice_in_dim(grad_out, row * d_panel, d_panel, 1).astype(jnp.float32).reshape(TOKENS, DPB, BLOCK)
        spots = lax.dynamic_index_in_dim(gate_slots, row, 0, keepdims=False)
        filled = lax.dynamic_index_in_dim(gate_count, row, 0, keepdims=False)
        down_spots = lax.dynamic_index_in_dim(down_slots, row, 0, keepdims=False)
        down_filled = lax.dynamic_index_in_dim(down_count, row, 0, keepdims=False)
        slot_ids = jnp.arange(NB, dtype=jnp.int32)[None, :]
        keep = (slot_ids < filled[:, None]).astype(jnp.float32)[:, :, None, None]
        down_keep = (slot_ids < down_filled[:, None]).astype(jnp.float32)[:, :, None, None]
        column_ids = jnp.arange(N_COL, dtype=jnp.int32)[:, None] * jnp.ones_like(spots)
        x_sel = x_panel[:, spots // FPB]
        gate_sel = gate_grid[:, column_ids, spots % FPB]
        up_sel = up_grid[:, column_ids, spots % FPB]
        grad_g = (jnp.einsum("tcnk,tcnj->cnkj", x_sel, gate_sel) * keep).astype(jnp.bfloat16)
        grad_u = (jnp.einsum("tcnk,tcnj->cnkj", x_sel, up_sel) * keep).astype(jnp.bfloat16)
        hid_sel = hid_grid[:, column_ids, down_spots % FPB]
        cot_sel = cot_panel[:, down_spots // FPB]
        grad_d = (jnp.einsum("tcnk,tcnj->cnkj", hid_sel, cot_sel) * down_keep).astype(jnp.bfloat16)
        return grad_g, grad_u, grad_d

    grad_gate_blocks, grad_up_blocks, grad_down_blocks = lax.map(block_grads, row_ids)
    return layer_out, grad_x, grad_gate_blocks, grad_up_blocks, grad_down_blocks
```

```python
import jax
import jax.numpy as jnp
from jax import lax
from jax.experimental import pallas as pl
from jax.experimental.pallas import tpu as pltpu
from jax.sharding import PartitionSpec as P

TOKENS = 256
BLOCK = 128
NB = 96
DPB = 8
FPB = 26
WIDTH = DPB * BLOCK
CHUNK = 2 * BLOCK
CHUNKS = FPB // 2
GROUP = 8
MESH = pl.DeviceIdType.MESH
F32 = jnp.float32
BF16 = jnp.bfloat16


def nt_dot(a, b):
    return lax.dot_general(a, b, (((1,), (1,)), ((), ())), preferred_element_type=F32)


def layer_kernel(
    gate_at,
    down_at,
    x_in,
    cot_in,
    gate_in,
    up_in,
    down_in,
    out_ref,
    gradx_ref,
    acts_out,
    xs_out,
    xs,
    raw_gate,
    raw_up,
    raw_down,
    w_gate,
    w_up,
    w_down,
    terms,
    half_al,
    half_ar,
    full_al,
    full_ar,
    sums,
    half_bl,
    half_br,
    full_bl,
    full_br,
    acts,
    out_acc,
    gradx_acc,
    tail,
    tail_core,
    tail_hl,
    tail_hr,
    tail_fl,
    tail_fr,
    load_sem,
    save_sem,
    head_send,
    head_recv,
    send_sem,
    recv_sem,
    tail_send,
    tail_recv,
):
    row, col = lax.axis_index("row"), lax.axis_index("col")
    z, y = row // 4, row % 4
    ix, core = col // 2, col % 2

    def y_dev(step):
        return (z * 4 + (y + step) % 4, col)

    def z_dev(step):
        return (((z + step) % 4) * 4 + y, col)

    def x_dev(step):
        return (row, ((ix + step) % 4) * 2 + core)

    sibling = (row, ix * 2 + 1 - core)

    loads = [
        pltpu.make_async_copy(x_in, xs.at[col, 0], load_sem.at[0]),
        pltpu.make_async_copy(cot_in, xs.at[col, 1], load_sem.at[1]),
        pltpu.make_async_copy(gate_in, raw_gate.at[pl.ds(0, NB)], load_sem.at[2]),
        pltpu.make_async_copy(up_in, raw_up.at[pl.ds(0, NB)], load_sem.at[3]),
        pltpu.make_async_copy(down_in, raw_down.at[pl.ds(0, NB)], load_sem.at[4]),
    ]
    for load in loads:
        load.start()

    barrier = pltpu.get_barrier_semaphore()
    for dev in (y_dev(1), y_dev(3), z_dev(1), z_dev(3), x_dev(1), x_dev(3), sibling):
        pl.semaphore_signal(barrier, inc=1, device_id=dev, device_id_type=MESH)

    zero = jnp.zeros((BLOCK, BLOCK), BF16)
    raw_gate[NB] = zero
    raw_up[NB] = zero
    raw_down[NB] = zero
    out_acc[...] = jnp.zeros_like(out_acc)
    gradx_acc[...] = jnp.zeros_like(gradx_acc)

    loads[0].wait()
    loads[1].wait()
    pl.semaphore_wait(barrier, 7)

    def head(n, ref, dev):
        return pltpu.make_async_remote_copy(
            src_ref=ref,
            dst_ref=ref,
            send_sem=head_send.at[n],
            recv_sem=head_recv.at[n],
            device_id=dev,
            device_id_type=MESH,
        )

    def at_x(step, side):
        return ((ix + step) % 4) * 2 + side

    other = 1 - core
    sent = []

    def head_start(n, ref, dev):
        copy = head(n, ref, dev)
        copy.start()
        sent.append(copy)

    head_start(0, xs.at[col], x_dev(1))
    head_start(1, xs.at[col], x_dev(3))
    head_start(2, xs.at[col], sibling)

    def place_gate(k, carry):
        for raw, dense in ((raw_gate, w_gate), (raw_up, w_up)):
            for r in range(DPB):
                for b in range(2):
                    slot = gate_at[r * FPB + 2 * k + b]
                    dense[k, r * BLOCK : (r + 1) * BLOCK, b * BLOCK : (b + 1) * BLOCK] = raw[slot]
        return carry

    def place_down(k, carry):
        for r in range(DPB):
            for b in range(2):
                slot = down_at[r * FPB + 2 * k + b]
                w_down[k, b * BLOCK : (b + 1) * BLOCK, r * BLOCK : (r + 1) * BLOCK] = raw_down[slot]
        return carry

    loads[2].wait()
    loads[3].wait()
    lax.fori_loop(0, 6, place_gate, 0)

    head(0, xs.at[at_x(3, core)], x_dev(1)).wait_recv()
    head_start(3, xs.at[at_x(3, core), 0], x_dev(1))
    head_start(4, xs.at[at_x(3, core)], sibling)
    head(1, xs.at[at_x(1, core)], x_dev(3)).wait_recv()
    head_start(5, xs.at[at_x(1, core), 1], x_dev(3))
    head_start(6, xs.at[at_x(1, core)], sibling)

    lax.fori_loop(6, CHUNKS, place_gate, 0)

    head(3, xs.at[at_x(2, core), 0], x_dev(1)).wait_recv()
    head_start(7, xs.at[at_x(2, core), 0], sibling)
    head(5, xs.at[at_x(2, core), 1], x_dev(3)).wait_recv()
    head_start(8, xs.at[at_x(2, core), 1], sibling)

    loads[4].wait()
    lax.fori_loop(0, CHUNKS, place_down, 0)

    head(2, xs.at[at_x(0, other)], sibling).wait_recv()
    head(4, xs.at[at_x(3, other)], sibling).wait_recv()
    head(6, xs.at[at_x(1, other)], sibling).wait_recv()
    head(7, xs.at[at_x(2, other), 0], sibling).wait_recv()
    head(8, xs.at[at_x(2, other), 1], sibling).wait_recv()
    save_xs = pltpu.make_async_copy(xs, xs_out, save_sem.at[CHUNKS])
    save_xs.start()

    def places(k):
        odd = k % 2
        i = (1 - odd) * y + odd * z
        j = (1 - odd) * z + odd * y

        def dev(step, along_z):
            y_new = (y + (1 - along_z) * step) % 4
            z_new = (z + along_z * step) % 4
            return (z_new * 4 + y_new, col)

        return i, j, dev(1, odd), dev(3, odd), dev(1, 1 - odd), dev(3, 1 - odd)

    def copy(k, n, src, dst, dev):
        return pltpu.make_async_remote_copy(
            src_ref=src,
            dst_ref=dst,
            send_sem=send_sem.at[k, n],
            recv_sem=recv_sem.at[k, n],
            device_id=dev,
            device_id_type=MESH,
        )

    def all_copies(k):
        i, j, ar, al, br, bl = places(k)
        i1, i2, i3 = (i + 1) % 4, (i + 2) % 4, (i + 3) % 4
        j1, j2, j3 = (j + 1) % 4, (j + 2) % 4, (j + 3) % 4
        same = lambda n, ref, dev: copy(k, n, ref, ref, dev)
        return [
            lambda: copy(k, 0, terms.at[k, i2, 0], half_al.at[k], ar),
            lambda: copy(k, 1, terms.at[k, i2, 1], half_ar.at[k], al),
            lambda: copy(k, 2, terms.at[k, i1], full_al.at[k], ar),
            lambda: copy(k, 3, terms.at[k, i3], full_ar.at[k], al),
            lambda: copy(k, 4, sums.at[k, j2, 0], half_bl.at[k], br),
            lambda: copy(k, 5, sums.at[k, j2, 1], half_br.at[k], bl),
            lambda: copy(k, 6, sums.at[k, j1], full_bl.at[k], br),
            lambda: copy(k, 7, sums.at[k, j3], full_br.at[k], bl),
            lambda: same(8, acts.at[k, i, j], br),
            lambda: same(9, acts.at[k, i, j], bl),
            lambda: same(10, acts.at[k, i, j3, 0], br),
            lambda: same(11, acts.at[k, i, j1, 1], bl),
            lambda: same(12, acts.at[k, i], ar),
            lambda: same(13, acts.at[k, i], al),
            lambda: same(14, acts.at[k, i3, pl.ds(0, 2)], ar),
            lambda: same(15, acts.at[k, i1, pl.ds(2, 2)], al),
        ]

    def arrived(k, n, ref):
        i, j, ar, al, br, bl = places(k)
        copy(k, n, ref, ref, ar).wait_recv()

    def plus(a, b):
        return (a.astype(F32) + b.astype(F32)).astype(BF16)

    def p0(k):
        for part, (arr, weights) in enumerate(((0, w_gate), (0, w_up), (1, w_down))):
            if part < 2:
                lhs = xs[:, 0].reshape(TOKENS, WIDTH)
                val = jnp.dot(lhs, weights[k], preferred_element_type=F32)
            else:
                lhs = xs[:, 1].reshape(TOKENS, WIDTH)
                val = nt_dot(lhs, weights[k])
            val = val.astype(BF16)
            for b in range(2):
                terms[k, :, b, :, part * 16 : (part + 1) * 16, :] = val[
                    :, b * BLOCK : (b + 1) * BLOCK
                ].reshape(4, 4, 16, BLOCK)
        copies = all_copies(k)
        copies[0]().start()
        copies[1]().start()

    def p1(k):
        i, j, *_ = places(k)
        i1, i3 = (i + 1) % 4, (i + 3) % 4
        copies = all_copies(k)
        arrived(k, 0, half_al.at[k])
        terms[k, i1, 0] = plus(terms[k, i1, 0], half_al[k])
        copies[2]().start()
        arrived(k, 1, half_ar.at[k])
        terms[k, i3, 1] = plus(terms[k, i3, 1], half_ar[k])
        copies[3]().start()

    def p2(k):
        i, j, *_ = places(k)
        copies = all_copies(k)
        arrived(k, 2, full_al.at[k])
        arrived(k, 3, full_ar.at[k])
        for b in range(2):
            total = terms[k, i, b].astype(F32) + full_al[k, b].astype(F32)
            sums[k, :, b] = (total + full_ar[k, b].astype(F32)).astype(BF16)
        copies[4]().start()
        copies[5]().start()

    def p3(k):
        i, j, *_ = places(k)
        j1, j3 = (j + 1) % 4, (j + 3) % 4
        copies = all_copies(k)
        arrived(k, 4, half_bl.at[k])
        sums[k, j1, 0] = plus(sums[k, j1, 0], half_bl[k])
        copies[6]().start()
        arrived(k, 5, half_br.at[k])
        sums[k, j3, 1] = plus(sums[k, j3, 1], half_br[k])
        copies[7]().start()

    def p4(k):
        i, j, *_ = places(k)
        copies = all_copies(k)
        arrived(k, 6, full_bl.at[k])
        arrived(k, 7, full_br.at[k])
        total = sums[k, j].astype(F32) + full_bl[k].astype(F32) + full_br[k].astype(F32)
        gate, up, grad = total[:, 0:16], total[:, 16:32], total[:, 32:48]
        sigma = 1.0 / (1.0 + jnp.exp(-gate))
        acts[k, i, j, :, 0:16, :] = (gate * sigma * up).astype(BF16)
        acts[k, i, j, :, 16:32, :] = (grad * up * sigma * (1.0 + gate * (1.0 - sigma))).astype(BF16)
        acts[k, i, j, :, 32:48, :] = (grad * gate * sigma).astype(BF16)
        copies[8]().start()
        copies[9]().start()

    def p5(k):
        i, j, *_ = places(k)
        copies = all_copies(k)
        arrived(k, 8, acts.at[k, i, (j + 3) % 4])
        copies[10]().start()
        arrived(k, 9, acts.at[k, i, (j + 1) % 4])
        copies[11]().start()

    def p6(k):
        i, j, *_ = places(k)
        copies = all_copies(k)
        arrived(k, 10, acts.at[k, i, (j + 2) % 4, 0])
        arrived(k, 11, acts.at[k, i, (j + 2) % 4, 1])
        copies[12]().start()
        copies[13]().start()

    def p7(k):
        i, j, *_ = places(k)
        copies = all_copies(k)
        arrived(k, 12, acts.at[k, (i + 3) % 4])
        copies[14]().start()
        arrived(k, 13, acts.at[k, (i + 1) % 4])
        copies[15]().start()

    def p8(k):
        i, j, *_ = places(k)
        arrived(k, 14, acts.at[k, (i + 2) % 4, pl.ds(0, 2)])
        arrived(k, 15, acts.at[k, (i + 2) % 4, pl.ds(2, 2)])
        pltpu.make_async_copy(acts.at[k], acts_out.at[k], save_sem.at[k]).start()

        def act(part):
            cols = [
                acts[k, :, :, b, part * 16 : (part + 1) * 16, :].reshape(TOKENS, BLOCK)
                for b in range(2)
            ]
            return jnp.concatenate(cols, axis=1)

        hidden, grad_gate, grad_up = act(0), act(1), act(2)
        for n in range(4):
            cols = slice(n * 256, (n + 1) * 256)
            out_acc[:, cols] += jnp.dot(hidden, w_down[k, :, cols], preferred_element_type=F32)
            gradx_acc[:, cols] += nt_dot(grad_gate, w_gate[k, cols, :]) + nt_dot(
                grad_up, w_up[k, cols, :]
            )
        for one in all_copies(k):
            one().wait_send()

    def tick(t, carry):
        for phase, late in ((p7, 7), (p6, 6), (p5, 5), (p4, 4), (p3, 3), (p2, 2), (p1, 1), (p0, 0), (p8, 8)):
            k = t - late

            @pl.when(jnp.logical_and(k >= 0, k < CHUNKS))
            def _():
                phase(k)

        return carry

    lax.fori_loop(0, CHUNKS + 8, tick, 0)

    for side in range(2):
        for at in range(4):
            rows = slice((at * 2 + side) * 32, (at * 2 + side + 1) * 32)
            tail[side, at, 0] = out_acc[rows, :].astype(BF16)
            tail[side, at, 1] = gradx_acc[rows, :].astype(BF16)

    def last(n, src, dst, dev):
        return pltpu.make_async_remote_copy(
            src_ref=src,
            dst_ref=dst,
            send_sem=tail_send.at[n],
            recv_sem=tail_recv.at[n],
            device_id=dev,
            device_id_type=MESH,
        )

    x0, x1, x2, x3 = ix, (ix + 1) % 4, (ix + 2) % 4, (ix + 3) % 4
    cores = {
        n: last(n, tail.at[other, at], tail_core.at[at], sibling)
        for n, at in ((0, x2), (1, x1), (2, x3), (3, x0))
    }
    for n in range(4):
        cores[n].start()
    right, left = x_dev(1), x_dev(3)
    cores[0].wait_recv()
    tail[core, x2] = plus(tail[core, x2], tail_core[x2])
    halves = [last(4, tail.at[core, x2, 0], tail_hl, right), last(5, tail.at[core, x2, 1], tail_hr, left)]
    for half in halves:
        half.start()
    cores[1].wait_recv()
    tail[core, x1] = plus(tail[core, x1], tail_core[x1])
    cores[2].wait_recv()
    tail[core, x3] = plus(tail[core, x3], tail_core[x3])
    fulls = [last(6, tail.at[core, x1], tail_fl, right), last(7, tail.at[core, x3], tail_fr, left)]
    halves[0].wait_recv()
    tail[core, x1, 0] = plus(tail[core, x1, 0], tail_hl[...])
    fulls[0].start()
    halves[1].wait_recv()
    tail[core, x3, 1] = plus(tail[core, x3, 1], tail_hr[...])
    fulls[1].start()
    cores[3].wait_recv()
    total = tail[core, x0].astype(F32) + tail_core[x0].astype(F32)
    fulls[0].wait_recv()
    fulls[1].wait_recv()
    total = total + tail_fl[...].astype(F32) + tail_fr[...].astype(F32)
    out_ref[...] = total[0].astype(BF16)
    gradx_ref[...] = total[1].astype(BF16)

    for one in sent + list(cores.values()) + halves + fulls:
        one.wait_send()
    save_xs.wait()

    def saved(k, carry):
        pltpu.make_async_copy(acts.at[k], acts_out.at[k], save_sem.at[k]).wait()
        return carry

    lax.fori_loop(0, CHUNKS, saved, 0)


def run_layer(gate_at, down_at, inputs, grad_out, gate_blocks, up_blocks, down_blocks):
    anywhere = pl.BlockSpec(memory_space=pl.ANY)
    scalars = pl.BlockSpec(memory_space=pltpu.SMEM)
    vmem = pl.BlockSpec(memory_space=pltpu.VMEM)
    raw = pltpu.VMEM((NB + 1, BLOCK, BLOCK), BF16)
    part = (48, BLOCK)
    return pl.pallas_call(
        layer_kernel,
        out_shape=(
            jax.ShapeDtypeStruct((32, WIDTH), BF16),
            jax.ShapeDtypeStruct((32, WIDTH), BF16),
            jax.ShapeDtypeStruct((CHUNKS, 4, 4, 2) + part, BF16),
            jax.ShapeDtypeStruct((8, 2, 32, WIDTH), BF16),
        ),
        in_specs=[scalars, scalars] + [anywhere] * 5,
        out_specs=(vmem, vmem, anywhere, anywhere),
        scratch_shapes=[
            pltpu.VMEM((8, 2, 32, WIDTH), BF16),
            raw,
            raw,
            raw,
            pltpu.VMEM((CHUNKS, WIDTH, CHUNK), BF16),
            pltpu.VMEM((CHUNKS, WIDTH, CHUNK), BF16),
            pltpu.VMEM((CHUNKS, CHUNK, WIDTH), BF16),
            pltpu.VMEM((CHUNKS, 4, 2, 4) + part, BF16),
            pltpu.VMEM((CHUNKS, 4) + part, BF16),
            pltpu.VMEM((CHUNKS, 4) + part, BF16),
            pltpu.VMEM((CHUNKS, 2, 4) + part, BF16),
            pltpu.VMEM((CHUNKS, 2, 4) + part, BF16),
            pltpu.VMEM((CHUNKS, 4, 2) + part, BF16),
            pltpu.VMEM((CHUNKS,) + part, BF16),
            pltpu.VMEM((CHUNKS,) + part, BF16),
            pltpu.VMEM((CHUNKS, 2) + part, BF16),
            pltpu.VMEM((CHUNKS, 2) + part, BF16),
            pltpu.VMEM((CHUNKS, 4, 4, 2) + part, BF16),
            pltpu.VMEM((TOKENS, WIDTH), F32),
            pltpu.VMEM((TOKENS, WIDTH), F32),
            pltpu.VMEM((2, 4, 2, 32, WIDTH), BF16),
            pltpu.VMEM((4, 2, 32, WIDTH), BF16),
            pltpu.VMEM((32, WIDTH), BF16),
            pltpu.VMEM((32, WIDTH), BF16),
            pltpu.VMEM((2, 32, WIDTH), BF16),
            pltpu.VMEM((2, 32, WIDTH), BF16),
            pltpu.SemaphoreType.DMA((5,)),
            pltpu.SemaphoreType.DMA((CHUNKS + 1,)),
            pltpu.SemaphoreType.DMA((9,)),
            pltpu.SemaphoreType.DMA((9,)),
            pltpu.SemaphoreType.DMA((CHUNKS, 16)),
            pltpu.SemaphoreType.DMA((CHUNKS, 16)),
            pltpu.SemaphoreType.DMA((8,)),
            pltpu.SemaphoreType.DMA((8,)),
        ],
        compiler_params=pltpu.CompilerParams(
            collective_id=0, has_side_effects=True, vmem_limit_bytes=60 * 2**20
        ),
        name="layer",
    )(gate_at, down_at, inputs, grad_out, gate_blocks, up_blocks, down_blocks)


def grads_kernel(
    gate_slots, down_slots, counts, acts, xs, gate_out, up_out, down_out, x_t, cots, pairs, hidden_t
):
    step = pl.program_id(0)

    @pl.when(step == 0)
    def _():
        for r in range(DPB):
            cols = slice(r * BLOCK, (r + 1) * BLOCK)
            x_t[r] = xs[:, 0, :, cols].reshape(TOKENS, BLOCK).T
            cots[r] = xs[:, 1, :, cols].reshape(TOKENS, BLOCK)

        def relay(k, carry):
            for b in range(2):
                act = [
                    acts[k, :, :, b, part * 16 : (part + 1) * 16, :].reshape(TOKENS, BLOCK)
                    for part in range(3)
                ]
                hidden_t[2 * k + b] = act[0].T
                pairs[2 * k + b, :, 0:BLOCK] = act[1]
                pairs[2 * k + b, :, BLOCK:] = act[2]
            return carry

        lax.fori_loop(0, CHUNKS, relay, 0)

    first = step * GROUP
    gate_live = counts[0] - first
    down_live = counts[1] - first

    @pl.when(gate_live > 0)
    def _():
        for u in range(GROUP):
            spot = gate_slots[first + u]
            both = jnp.dot(x_t[spot // FPB], pairs[spot % FPB], preferred_element_type=F32)
            both = jnp.where(u < gate_live, both, 0.0).astype(BF16)
            gate_out[u] = both[:, 0:BLOCK]
            up_out[u] = both[:, BLOCK:]

    @pl.when(gate_live <= 0)
    def _():
        gate_out[...] = jnp.zeros_like(gate_out)
        up_out[...] = jnp.zeros_like(up_out)

    @pl.when(down_live > 0)
    def _():
        for u in range(GROUP):
            spot = down_slots[first + u]
            val = jnp.dot(hidden_t[spot % FPB], cots[spot // FPB], preferred_element_type=F32)
            down_out[u] = jnp.where(u < down_live, val, 0.0).astype(BF16)

    @pl.when(down_live <= 0)
    def _():
        down_out[...] = jnp.zeros_like(down_out)


def run_grads(gate_slots, down_slots, counts, acts, xs):
    scalars = pl.BlockSpec(memory_space=pltpu.SMEM)
    whole = pl.BlockSpec(memory_space=pltpu.VMEM)
    blocks = pl.BlockSpec((GROUP, BLOCK, BLOCK), lambda s: (s, 0, 0))
    grads = jax.ShapeDtypeStruct((NB, BLOCK, BLOCK), BF16)
    return pl.pallas_call(
        grads_kernel,
        grid=(NB // GROUP,),
        out_shape=(grads, grads, grads),
        in_specs=[scalars, scalars, scalars, whole, whole],
        out_specs=(blocks, blocks, blocks),
        scratch_shapes=[
            pltpu.VMEM((DPB, BLOCK, TOKENS), BF16),
            pltpu.VMEM((DPB, TOKENS, BLOCK), BF16),
            pltpu.VMEM((FPB, TOKENS, 2 * BLOCK), BF16),
            pltpu.VMEM((FPB, BLOCK, TOKENS), BF16),
        ],
        compiler_params=pltpu.CompilerParams(vmem_limit_bytes=40 * 2**20),
        name="block_grads",
    )(gate_slots, down_slots, counts, acts, xs)


def slot_of(slots, count):
    ids = jnp.arange(NB, dtype=jnp.int32)
    spots = jnp.arange(DPB * FPB, dtype=jnp.int32)
    hit = (slots[None, :] == spots[:, None]) & (ids < count)[None, :]
    return jnp.min(jnp.where(hit, ids[None, :], NB), axis=1)


def local(
    inputs,
    grad_out,
    gate_blocks,
    up_blocks,
    down_blocks,
    gate_slots,
    gate_count,
    down_slots,
    down_count,
):
    gate_slots, down_slots = gate_slots[0, 0], down_slots[0, 0]
    gate_count, down_count = gate_count[0, 0], down_count[0, 0]
    layer_out, grad_x, acts, xs = run_layer(
        slot_of(gate_slots, gate_count),
        slot_of(down_slots, down_count),
        inputs,
        grad_out,
        gate_blocks[0, 0],
        up_blocks[0, 0],
        down_blocks[0, 0],
    )
    counts = jnp.stack([gate_count, down_count])
    grads = run_grads(gate_slots, down_slots, counts, acts, xs)
    return (layer_out, grad_x) + tuple(grad[None, None] for grad in grads)


def solution(mesh):
    tokens = P("col", "row")
    blocks = P("row", "col", None, None, None)
    slots = P("row", "col", None)
    count = P("row", "col")
    return jax.shard_map(
        local,
        mesh=mesh,
        in_specs=(tokens, tokens, blocks, blocks, blocks, slots, count, slots, count),
        out_specs=(tokens, tokens, blocks, blocks, blocks),
        check_vma=False,
    )
```

```python
import jax
import jax.numpy as jnp
from jax import lax
from jax.experimental import pallas as pl
from jax.experimental.pallas import tpu as pltpu
from jax.sharding import PartitionSpec as P

TOKENS = 256
BLOCK = 128
NB = 96
DPB = 8
FPB = 26
WIDTH = DPB * BLOCK
CHUNK = 2 * BLOCK
CHUNKS = FPB // 2
GROUP = 16
LAGS = (0, 4, 8, 12, 16, 20, 24, 28, 32)
MESH = pl.DeviceIdType.MESH
F32 = jnp.float32
BF16 = jnp.bfloat16


def nt_dot(a, b):
    return lax.dot_general(a, b, (((1,), (1,)), ((), ())), preferred_element_type=F32)


def layer_kernel(
    gate_at,
    down_at,
    x_in,
    cot_in,
    gate_in,
    up_in,
    down_in,
    layer_ref,
    hidden_out,
    pairs_out,
    x_out,
    cots_out,
    xs,
    raw_gate,
    raw_up,
    raw_down,
    w_gate,
    w_up,
    w_down,
    terms,
    half_al,
    half_ar,
    full_al,
    full_ar,
    sums,
    half_bl,
    half_br,
    full_bl,
    full_br,
    acts,
    hidden_t,
    pairs,
    x_t,
    cots,
    out_acc,
    gradx_acc,
    tail,
    tail_out,
    tail_core,
    tail_hl,
    tail_hr,
    tail_fl,
    tail_fr,
    load_sem,
    save_sem,
    head_send,
    head_recv,
    send_sem,
    recv_sem,
    tail_send,
    tail_recv,
):
    row, col = lax.axis_index("row"), lax.axis_index("col")
    z, y = row // 4, row % 4
    ix, core = col // 2, col % 2

    def y_dev(step):
        return (z * 4 + (y + step) % 4, col)

    def z_dev(step):
        return (((z + step) % 4) * 4 + y, col)

    def x_dev(step):
        return (row, ((ix + step) % 4) * 2 + core)

    sibling = (row, ix * 2 + 1 - core)

    loads = [
        pltpu.make_async_copy(x_in, xs.at[col, 0], load_sem.at[0]),
        pltpu.make_async_copy(cot_in, xs.at[col, 1], load_sem.at[1]),
        pltpu.make_async_copy(gate_in, raw_gate.at[pl.ds(0, NB)], load_sem.at[2]),
        pltpu.make_async_copy(up_in, raw_up.at[pl.ds(0, NB)], load_sem.at[3]),
        pltpu.make_async_copy(down_in, raw_down.at[pl.ds(0, NB)], load_sem.at[4]),
    ]
    for load in loads:
        load.start()

    barrier = pltpu.get_barrier_semaphore()
    for dev in (y_dev(1), y_dev(3), z_dev(1), z_dev(3), x_dev(1), x_dev(3), sibling):
        pl.semaphore_signal(barrier, inc=1, device_id=dev, device_id_type=MESH)

    zero = jnp.zeros((BLOCK, BLOCK), BF16)
    raw_gate[NB] = zero
    raw_up[NB] = zero
    raw_down[NB] = zero
    out_acc[...] = jnp.zeros_like(out_acc)
    gradx_acc[...] = jnp.zeros_like(gradx_acc)

    pl.semaphore_wait(barrier, 7)

    def head(n, src, dst, dev):
        return pltpu.make_async_remote_copy(
            src_ref=src,
            dst_ref=dst,
            send_sem=head_send.at[n],
            recv_sem=head_recv.at[n],
            device_id=dev,
            device_id_type=MESH,
        )

    other = 1 - core
    right, left = x_dev(1), x_dev(3)
    sent = []

    def at_x(step, side, arr):
        return xs.at[((ix + step) % 4) * 2 + side, arr]

    def head_start(n, src, dst, dev):
        one = head(n, src, dst, dev)
        one.start()
        sent.append(one)

    def forward(n, ref, dev):
        head_start(n, ref, ref, dev)

    def head_wait(n, ref):
        head(n, ref, ref, right).wait_recv()

    head_start(0, x_in, xs.at[col, 0], right)
    head_start(1, cot_in, xs.at[col, 1], left)
    head_start(2, cot_in, xs.at[col, 1], right)
    head_start(3, x_in, xs.at[col, 0], left)
    head_start(4, x_in, xs.at[col, 0], sibling)
    head_start(5, cot_in, xs.at[col, 1], sibling)

    def place_gate(k, carry):
        for raw, dense in ((raw_gate, w_gate), (raw_up, w_up)):
            for r in range(DPB):
                for b in range(2):
                    slot = gate_at[r * FPB + 2 * k + b]
                    dense[k, r * BLOCK : (r + 1) * BLOCK, b * BLOCK : (b + 1) * BLOCK] = raw[slot]
        return carry

    def place_down(k, carry):
        for r in range(DPB):
            for b in range(2):
                slot = down_at[r * FPB + 2 * k + b]
                w_down[k, b * BLOCK : (b + 1) * BLOCK, r * BLOCK : (r + 1) * BLOCK] = raw_down[slot]
        return carry

    loads[2].wait()
    loads[3].wait()
    lax.fori_loop(0, 4, place_gate, 0)

    head_wait(0, at_x(3, core, 0))
    forward(6, at_x(3, core, 0), right)
    forward(7, at_x(3, core, 0), sibling)
    head_wait(1, at_x(1, core, 1))
    forward(8, at_x(1, core, 1), left)
    forward(9, at_x(1, core, 1), sibling)

    lax.fori_loop(4, 8, place_gate, 0)

    head_wait(2, at_x(3, core, 1))
    forward(10, at_x(3, core, 1), sibling)
    head_wait(3, at_x(1, core, 0))
    forward(11, at_x(1, core, 0), sibling)

    lax.fori_loop(8, CHUNKS, place_gate, 0)
    loads[4].wait()
    lax.fori_loop(0, 4, place_down, 0)

    head_wait(6, at_x(2, core, 0))
    forward(12, at_x(2, core, 0), sibling)
    head_wait(8, at_x(2, core, 1))
    forward(13, at_x(2, core, 1), sibling)

    lax.fori_loop(4, CHUNKS, place_down, 0)

    head_wait(4, at_x(0, other, 0))
    head_wait(5, at_x(0, other, 1))
    head_wait(7, at_x(3, other, 0))
    head_wait(9, at_x(1, other, 1))
    head_wait(10, at_x(3, other, 1))
    head_wait(11, at_x(1, other, 0))
    head_wait(12, at_x(2, other, 0))
    head_wait(13, at_x(2, other, 1))
    loads[0].wait()
    loads[1].wait()

    save_x = pltpu.make_async_copy(x_t, x_out, save_sem.at[2 * CHUNKS])
    save_cots = pltpu.make_async_copy(cots, cots_out, save_sem.at[2 * CHUNKS + 1])

    def lay_out_inputs():
        for r in range(DPB):
            cols = slice(r * BLOCK, (r + 1) * BLOCK)
            x_t[r] = xs[:, 0, :, cols].reshape(TOKENS, BLOCK).T
            cots[r] = xs[:, 1, :, cols].reshape(TOKENS, BLOCK)
        save_x.start()
        save_cots.start()

    def places(k):
        odd = k % 2
        i = (1 - odd) * y + odd * z
        j = (1 - odd) * z + odd * y

        def dev(step, along_z):
            y_new = (y + (1 - along_z) * step) % 4
            z_new = (z + along_z * step) % 4
            return (z_new * 4 + y_new, col)

        return i, j, dev(1, odd), dev(3, odd), dev(1, 1 - odd), dev(3, 1 - odd)

    def copy(k, n, src, dst, dev):
        return pltpu.make_async_remote_copy(
            src_ref=src,
            dst_ref=dst,
            send_sem=send_sem.at[k, n],
            recv_sem=recv_sem.at[k, n],
            device_id=dev,
            device_id_type=MESH,
        )

    def all_copies(k):
        i, j, ar, al, br, bl = places(k)
        i1, i2, i3 = (i + 1) % 4, (i + 2) % 4, (i + 3) % 4
        j1, j2, j3 = (j + 1) % 4, (j + 2) % 4, (j + 3) % 4
        same = lambda n, ref, dev: copy(k, n, ref, ref, dev)
        near, far = pl.ds(0, 2), pl.ds(2, 2)
        return [
            lambda: copy(k, 0, terms.at[k, i2, 0], half_al.at[k], ar),
            lambda: copy(k, 1, terms.at[k, i2, 1], half_ar.at[k], al),
            lambda: copy(k, 2, terms.at[k, i1, 1], full_al.at[k, 1], ar),
            lambda: copy(k, 3, terms.at[k, i3, 0], full_ar.at[k, 0], al),
            lambda: copy(k, 4, terms.at[k, i1, 0], full_al.at[k, 0], ar),
            lambda: copy(k, 5, terms.at[k, i3, 1], full_ar.at[k, 1], al),
            lambda: copy(k, 6, sums.at[k, j2, 0], half_bl.at[k], br),
            lambda: copy(k, 7, sums.at[k, j2, 1], half_br.at[k], bl),
            lambda: copy(k, 8, sums.at[k, j1], full_bl.at[k], br),
            lambda: copy(k, 9, sums.at[k, j3], full_br.at[k], bl),
            lambda: same(10, acts.at[k, i, j], br),
            lambda: same(11, acts.at[k, i, j], bl),
            lambda: same(12, acts.at[k, i, j3, 0], br),
            lambda: same(13, acts.at[k, i, j1, 1], bl),
            lambda: same(14, acts.at[k, i, near], ar),
            lambda: same(15, acts.at[k, i, far], al),
            lambda: same(16, acts.at[k, i, far], ar),
            lambda: same(17, acts.at[k, i, near], al),
            lambda: same(18, acts.at[k, i3, near], ar),
            lambda: same(19, acts.at[k, i1, far], al),
        ]

    def arrived(k, n, ref):
        i, j, ar, al, br, bl = places(k)
        copy(k, n, ref, ref, ar).wait_recv()

    def plus(a, b):
        return (a.astype(F32) + b.astype(F32)).astype(BF16)

    def p0(k):
        for part, (arr, weights) in enumerate(((0, w_gate), (0, w_up), (1, w_down))):
            if part < 2:
                lhs = xs[:, 0].reshape(TOKENS, WIDTH)
                val = jnp.dot(lhs, weights[k], preferred_element_type=F32)
            else:
                lhs = xs[:, 1].reshape(TOKENS, WIDTH)
                val = nt_dot(lhs, weights[k])
            val = val.astype(BF16)
            for b in range(2):
                terms[k, :, b, :, part * 16 : (part + 1) * 16, :] = val[
                    :, b * BLOCK : (b + 1) * BLOCK
                ].reshape(4, 4, 16, BLOCK)
        copies = all_copies(k)
        for n in range(4):
            copies[n]().start()

    def p1(k):
        i, j, *_ = places(k)
        i1, i3 = (i + 1) % 4, (i + 3) % 4
        copies = all_copies(k)
        arrived(k, 0, half_al.at[k])
        terms[k, i1, 0] = plus(terms[k, i1, 0], half_al[k])
        copies[4]().start()
        arrived(k, 1, half_ar.at[k])
        terms[k, i3, 1] = plus(terms[k, i3, 1], half_ar[k])
        copies[5]().start()

    def p2(k):
        i, j, *_ = places(k)
        copies = all_copies(k)
        arrived(k, 2, full_al.at[k, 1])
        arrived(k, 3, full_ar.at[k, 0])
        arrived(k, 4, full_al.at[k, 0])
        arrived(k, 5, full_ar.at[k, 1])
        for b in range(2):
            total = terms[k, i, b].astype(F32) + full_al[k, b].astype(F32)
            sums[k, :, b] = (total + full_ar[k, b].astype(F32)).astype(BF16)
        copies[6]().start()
        copies[7]().start()

    def p3(k):
        i, j, *_ = places(k)
        j1, j3 = (j + 1) % 4, (j + 3) % 4
        copies = all_copies(k)
        arrived(k, 6, half_bl.at[k])
        sums[k, j1, 0] = plus(sums[k, j1, 0], half_bl[k])
        copies[8]().start()
        arrived(k, 7, half_br.at[k])
        sums[k, j3, 1] = plus(sums[k, j3, 1], half_br[k])
        copies[9]().start()

    def p4(k):
        i, j, *_ = places(k)
        copies = all_copies(k)
        arrived(k, 8, full_bl.at[k])
        arrived(k, 9, full_br.at[k])
        total = sums[k, j].astype(F32) + full_bl[k].astype(F32) + full_br[k].astype(F32)
        gate, up, grad = total[:, 0:16], total[:, 16:32], total[:, 32:48]
        sigma = 1.0 / (1.0 + jnp.exp(-gate))
        acts[k, i, j, :, 0:16, :] = (gate * sigma * up).astype(BF16)
        acts[k, i, j, :, 16:32, :] = (grad * up * sigma * (1.0 + gate * (1.0 - sigma))).astype(BF16)
        acts[k, i, j, :, 32:48, :] = (grad * gate * sigma).astype(BF16)
        copies[10]().start()
        copies[11]().start()

    def p5(k):
        i, j, *_ = places(k)
        copies = all_copies(k)
        arrived(k, 10, acts.at[k, i, (j + 3) % 4])
        copies[12]().start()
        arrived(k, 11, acts.at[k, i, (j + 1) % 4])
        copies[13]().start()

    def p6(k):
        i, j, *_ = places(k)
        copies = all_copies(k)
        arrived(k, 12, acts.at[k, i, (j + 2) % 4, 0])
        arrived(k, 13, acts.at[k, i, (j + 2) % 4, 1])
        for n in range(14, 18):
            copies[n]().start()

    def p7(k):
        i, j, *_ = places(k)
        copies = all_copies(k)
        arrived(k, 14, acts.at[k, (i + 3) % 4, pl.ds(0, 2)])
        copies[18]().start()
        arrived(k, 15, acts.at[k, (i + 1) % 4, pl.ds(2, 2)])
        copies[19]().start()

    def saves(k):
        return (
            pltpu.make_async_copy(hidden_t.at[k], hidden_out.at[k], save_sem.at[2 * k]),
            pltpu.make_async_copy(pairs.at[k], pairs_out.at[k], save_sem.at[2 * k + 1]),
        )

    def p8(k):
        i, j, *_ = places(k)
        arrived(k, 16, acts.at[k, (i + 3) % 4, pl.ds(2, 2)])
        arrived(k, 17, acts.at[k, (i + 1) % 4, pl.ds(0, 2)])
        arrived(k, 18, acts.at[k, (i + 2) % 4, pl.ds(0, 2)])
        arrived(k, 19, acts.at[k, (i + 2) % 4, pl.ds(2, 2)])

        def act(part):
            cols = [
                acts[k, :, :, b, part * 16 : (part + 1) * 16, :].reshape(TOKENS, BLOCK)
                for b in range(2)
            ]
            return cols, jnp.concatenate(cols, axis=1)

        (_, hidden), (gate_cols, grad_gate), (up_cols, grad_up) = act(0), act(1), act(2)
        for n in range(4):
            cols = slice(n * 256, (n + 1) * 256)
            out = jnp.dot(hidden, w_down[k, :, cols], preferred_element_type=F32)
            out_acc[:, :, cols] += out.reshape(8, 32, 256)
            grad = nt_dot(grad_gate, w_gate[k, cols, :]) + nt_dot(grad_up, w_up[k, cols, :])
            gradx_acc[:, :, cols] += grad.reshape(8, 32, 256)
        hidden_t[k] = hidden.T
        for b in range(2):
            pairs[k, b, :, 0:BLOCK] = gate_cols[b]
            pairs[k, b, :, BLOCK:] = up_cols[b]
        for save in saves(k):
            save.start()
        for one in all_copies(k):
            one().wait_send()

    def tick(t, carry):
        for phase, late in zip((p7, p6, p5, p4, p3, p2, p1, p0, p8), LAGS[7::-1] + LAGS[8:]):
            k = t - late

            @pl.when(jnp.logical_and(k >= 0, k < CHUNKS))
            def _():
                phase(k)

        @pl.when(t == 6)
        def _():
            lay_out_inputs()

        return carry

    lax.fori_loop(0, CHUNKS + LAGS[8], tick, 0)

    def last(n, src, dst, dev):
        return pltpu.make_async_remote_copy(
            src_ref=src,
            dst_ref=dst,
            send_sem=tail_send.at[n],
            recv_sem=tail_recv.at[n],
            device_id=dev,
            device_id_type=MESH,
        )

    x0, x1, x2, x3 = ix, (ix + 1) % 4, (ix + 2) % 4, (ix + 3) % 4
    totals = (out_acc, gradx_acc)
    cores = {}
    for n, at in ((0, x2), (1, x1), (2, x3), (3, x0)):
        for arr in range(2):
            tail_out[at, arr] = totals[arr][at * 2 + other].astype(BF16)
        cores[n] = last(n, tail_out.at[at], tail_core.at[at], sibling)
        cores[n].start()

    def both(n, at):
        cores[n].wait_recv()
        for arr in range(2):
            mine = totals[arr][at * 2 + core] + tail_core[at, arr].astype(F32)
            tail[at, arr] = mine.astype(BF16)

    steps = [
        last(4, tail.at[x2, 0], tail_hl, right),
        last(5, tail.at[x2, 1], tail_hr, left),
        last(6, tail.at[x1, 1], tail_fl.at[1], right),
        last(7, tail.at[x3, 0], tail_fr.at[0], left),
        last(8, tail.at[x1, 0], tail_fl.at[0], right),
        last(9, tail.at[x3, 1], tail_fr.at[1], left),
    ]
    both(0, x2)
    steps[0].start()
    steps[1].start()
    both(1, x1)
    steps[2].start()
    both(2, x3)
    steps[3].start()
    steps[0].wait_recv()
    tail[x1, 0] = plus(tail[x1, 0], tail_hl[...])
    steps[4].start()
    steps[1].wait_recv()
    tail[x3, 1] = plus(tail[x3, 1], tail_hr[...])
    steps[5].start()
    cores[3].wait_recv()
    for n in (2, 3, 4, 5):
        steps[n].wait_recv()
    for arr in range(2):
        total = totals[arr][x0 * 2 + core] + tail_core[x0, arr].astype(F32)
        total = total + tail_fl[arr].astype(F32) + tail_fr[arr].astype(F32)
        layer_ref[arr] = total.astype(BF16)

    for one in sent + list(cores.values()) + steps:
        one.wait_send()
    save_x.wait()
    save_cots.wait()

    def saved(k, carry):
        for save in saves(k):
            save.wait()
        return carry

    lax.fori_loop(0, CHUNKS, saved, 0)


def run_layer(gate_at, down_at, inputs, grad_out, gate_blocks, up_blocks, down_blocks):
    anywhere = pl.BlockSpec(memory_space=pl.ANY)
    scalars = pl.BlockSpec(memory_space=pltpu.SMEM)
    vmem = pl.BlockSpec(memory_space=pltpu.VMEM)
    raw = pltpu.VMEM((NB + 1, BLOCK, BLOCK), BF16)
    part = (48, BLOCK)
    return pl.pallas_call(
        layer_kernel,
        out_shape=(
            jax.ShapeDtypeStruct((2, 32, WIDTH), BF16),
            jax.ShapeDtypeStruct((CHUNKS, CHUNK, TOKENS), BF16),
            jax.ShapeDtypeStruct((CHUNKS, 2, TOKENS, 2 * BLOCK), BF16),
            jax.ShapeDtypeStruct((DPB, BLOCK, TOKENS), BF16),
            jax.ShapeDtypeStruct((DPB, TOKENS, BLOCK), BF16),
        ),
        in_specs=[scalars, scalars] + [anywhere] * 5,
        out_specs=(vmem, anywhere, anywhere, anywhere, anywhere),
        scratch_shapes=[
            pltpu.VMEM((8, 2, 32, WIDTH), BF16),
            raw,
            raw,
            raw,
            pltpu.VMEM((CHUNKS, WIDTH, CHUNK), BF16),
            pltpu.VMEM((CHUNKS, WIDTH, CHUNK), BF16),
            pltpu.VMEM((CHUNKS, CHUNK, WIDTH), BF16),
            pltpu.VMEM((CHUNKS, 4, 2, 4) + part, BF16),
            pltpu.VMEM((CHUNKS, 4) + part, BF16),
            pltpu.VMEM((CHUNKS, 4) + part, BF16),
            pltpu.VMEM((CHUNKS, 2, 4) + part, BF16),
            pltpu.VMEM((CHUNKS, 2, 4) + part, BF16),
            pltpu.VMEM((CHUNKS, 4, 2) + part, BF16),
            pltpu.VMEM((CHUNKS,) + part, BF16),
            pltpu.VMEM((CHUNKS,) + part, BF16),
            pltpu.VMEM((CHUNKS, 2) + part, BF16),
            pltpu.VMEM((CHUNKS, 2) + part, BF16),
            pltpu.VMEM((CHUNKS, 4, 4, 2) + part, BF16),
            pltpu.VMEM((CHUNKS, CHUNK, TOKENS), BF16),
            pltpu.VMEM((CHUNKS, 2, TOKENS, 2 * BLOCK), BF16),
            pltpu.VMEM((DPB, BLOCK, TOKENS), BF16),
            pltpu.VMEM((DPB, TOKENS, BLOCK), BF16),
            pltpu.VMEM((8, 32, WIDTH), F32),
            pltpu.VMEM((8, 32, WIDTH), F32),
            pltpu.VMEM((4, 2, 32, WIDTH), BF16),
            pltpu.VMEM((4, 2, 32, WIDTH), BF16),
            pltpu.VMEM((4, 2, 32, WIDTH), BF16),
            pltpu.VMEM((32, WIDTH), BF16),
            pltpu.VMEM((32, WIDTH), BF16),
            pltpu.VMEM((2, 32, WIDTH), BF16),
            pltpu.VMEM((2, 32, WIDTH), BF16),
            pltpu.SemaphoreType.DMA((5,)),
            pltpu.SemaphoreType.DMA((2 * CHUNKS + 2,)),
            pltpu.SemaphoreType.DMA((14,)),
            pltpu.SemaphoreType.DMA((14,)),
            pltpu.SemaphoreType.DMA((CHUNKS, 20)),
            pltpu.SemaphoreType.DMA((CHUNKS, 20)),
            pltpu.SemaphoreType.DMA((10,)),
            pltpu.SemaphoreType.DMA((10,)),
        ],
        compiler_params=pltpu.CompilerParams(
            collective_id=0, has_side_effects=True, vmem_limit_bytes=60 * 2**20
        ),
        name="layer",
    )(gate_at, down_at, inputs, grad_out, gate_blocks, up_blocks, down_blocks)


def grads_kernel(
    gate_slots,
    down_slots,
    counts,
    layer_in,
    hidden_in,
    pairs_in,
    x_in,
    cots_in,
    out_ref,
    gradx_ref,
    gate_out,
    up_out,
    down_out,
    hidden_t,
    pairs,
    x_t,
    cots,
    gate_stage,
    up_stage,
    down_stage,
    load_sem,
    save_sem,
):
    loads = [
        pltpu.make_async_copy(cots_in, cots, load_sem.at[0]),
        pltpu.make_async_copy(hidden_in, hidden_t, load_sem.at[1]),
        pltpu.make_async_copy(x_in, x_t, load_sem.at[2]),
        pltpu.make_async_copy(pairs_in, pairs, load_sem.at[3]),
    ]
    for load in loads:
        load.start()
    out_ref[...] = layer_in[0]
    gradx_ref[...] = layer_in[1]
    groups = NB // GROUP

    def save(kind, stage, out, g):
        rows = pl.ds(g * GROUP, GROUP)
        return pltpu.make_async_copy(stage.at[rows], out.at[rows], save_sem.at[kind, g])

    loads[0].wait()
    loads[1].wait()

    def down_group(g, carry):
        first = g * GROUP
        live = counts[1] - first

        @pl.when(live > 0)
        def _():
            for u in range(GROUP):
                spot = down_slots[first + u]
                val = jnp.dot(hidden_t[spot % FPB], cots[spot // FPB], preferred_element_type=F32)
                down_stage[first + u] = jnp.where(u < live, val, 0.0).astype(BF16)

        @pl.when(live <= 0)
        def _():
            down_stage[pl.ds(first, GROUP)] = jnp.zeros((GROUP, BLOCK, BLOCK), BF16)

        save(0, down_stage, down_out, g).start()
        return carry

    lax.fori_loop(0, groups, down_group, 0)
    loads[2].wait()
    loads[3].wait()

    def gate_group(g, carry):
        first = g * GROUP
        live = counts[0] - first

        @pl.when(live > 0)
        def _():
            for u in range(GROUP):
                spot = gate_slots[first + u]
                val = jnp.dot(x_t[spot // FPB], pairs[spot % FPB], preferred_element_type=F32)
                val = jnp.where(u < live, val, 0.0).astype(BF16)
                gate_stage[first + u] = val[:, 0:BLOCK]
                up_stage[first + u] = val[:, BLOCK:]

        @pl.when(live <= 0)
        def _():
            zero = jnp.zeros((GROUP, BLOCK, BLOCK), BF16)
            gate_stage[pl.ds(first, GROUP)] = zero
            up_stage[pl.ds(first, GROUP)] = zero

        save(1, gate_stage, gate_out, g).start()
        save(2, up_stage, up_out, g).start()
        return carry

    lax.fori_loop(0, groups, gate_group, 0)

    def finish(g, carry):
        save(0, down_stage, down_out, g).wait()
        save(1, gate_stage, gate_out, g).wait()
        save(2, up_stage, up_out, g).wait()
        return carry

    lax.fori_loop(0, groups, finish, 0)


def run_grads(gate_slots, down_slots, counts, layer, hidden, pairs, x_t, cots):
    scalars = pl.BlockSpec(memory_space=pltpu.SMEM)
    vmem = pl.BlockSpec(memory_space=pltpu.VMEM)
    anywhere = pl.BlockSpec(memory_space=pl.ANY)
    grads = jax.ShapeDtypeStruct((NB, BLOCK, BLOCK), BF16)
    tokens = jax.ShapeDtypeStruct((32, WIDTH), BF16)
    return pl.pallas_call(
        grads_kernel,
        out_shape=(tokens, tokens, grads, grads, grads),
        in_specs=[scalars, scalars, scalars, vmem] + [anywhere] * 4,
        out_specs=(vmem, vmem, anywhere, anywhere, anywhere),
        scratch_shapes=[
            pltpu.VMEM((FPB, BLOCK, TOKENS), BF16),
            pltpu.VMEM((FPB, TOKENS, 2 * BLOCK), BF16),
            pltpu.VMEM((DPB, BLOCK, TOKENS), BF16),
            pltpu.VMEM((DPB, TOKENS, BLOCK), BF16),
            pltpu.VMEM((NB, BLOCK, BLOCK), BF16),
            pltpu.VMEM((NB, BLOCK, BLOCK), BF16),
            pltpu.VMEM((NB, BLOCK, BLOCK), BF16),
            pltpu.SemaphoreType.DMA((4,)),
            pltpu.SemaphoreType.DMA((3, NB // GROUP)),
        ],
        compiler_params=pltpu.CompilerParams(vmem_limit_bytes=60 * 2**20),
        name="block_grads",
    )(gate_slots, down_slots, counts, layer, hidden, pairs, x_t, cots)


def slot_of(slots, count):
    ids = jnp.arange(NB, dtype=jnp.int32)
    spots = jnp.arange(DPB * FPB, dtype=jnp.int32)
    hit = (slots[None, :] == spots[:, None]) & (ids < count)[None, :]
    return jnp.min(jnp.where(hit, ids[None, :], NB), axis=1)


def local(
    inputs,
    grad_out,
    gate_blocks,
    up_blocks,
    down_blocks,
    gate_slots,
    gate_count,
    down_slots,
    down_count,
):
    gate_slots, down_slots = gate_slots[0, 0], down_slots[0, 0]
    gate_count, down_count = gate_count[0, 0], down_count[0, 0]
    layer, hidden, pairs, x_t, cots = run_layer(
        slot_of(gate_slots, gate_count),
        slot_of(down_slots, down_count),
        inputs,
        grad_out,
        gate_blocks[0, 0],
        up_blocks[0, 0],
        down_blocks[0, 0],
    )
    counts = jnp.stack([gate_count, down_count])
    hidden = hidden.reshape(FPB, BLOCK, TOKENS)
    pairs = pairs.reshape(FPB, TOKENS, 2 * BLOCK)
    layer_out, grad_x, *grads = run_grads(
        gate_slots, down_slots, counts, layer, hidden, pairs, x_t, cots
    )
    return (layer_out, grad_x) + tuple(grad[None, None] for grad in grads)


def solution(mesh):
    tokens = P("col", "row")
    blocks = P("row", "col", None, None, None)
    slots = P("row", "col", None)
    count = P("row", "col")
    return jax.shard_map(
        local,
        mesh=mesh,
        in_specs=(tokens, tokens, blocks, blocks, blocks, slots, count, slots, count),
        out_specs=(tokens, tokens, blocks, blocks, blocks),
        check_vma=False,
    )
```

```python
import jax
import jax.numpy as jnp
from jax import lax
from jax.experimental import pallas as pl
from jax.experimental.pallas import tpu as pltpu
from jax.sharding import PartitionSpec as P

TOKENS = 256
BLOCK = 128
NB = 96
DPB = 8
FPB = 26
WIDTH = DPB * BLOCK
CHUNK = 2 * BLOCK
CHUNKS = FPB // 2
GROUP = 16
LAGS = (0, 4, 8, 12, 16, 20, 24, 28, 32)
MESH = pl.DeviceIdType.MESH
HEAD_SEM = (0, 1, 2, 3, 6, 6, 4, 6, 5, 6, 6, 6, 6, 6)
SEND_SEM = (0,) * 6 + (1,) * 8 + (2,) * 6
RECV_SEM = (0, 0, 1, 1, 1, 1, 2, 2, 3, 3, 4, 4, 5, 5, 6, 6, 7, 7, 7, 7)
F32 = jnp.float32
BF16 = jnp.bfloat16


def nt_dot(a, b):
    return lax.dot_general(a, b, (((1,), (1,)), ((), ())), preferred_element_type=F32)


def layer_kernel(
    gate_slots,
    gate_count,
    down_slots,
    down_count,
    x_in,
    cot_in,
    gate_in,
    up_in,
    down_in,
    part1_ref,
    part2_ref,
    part3_ref,
    mine_ref,
    hidden_out,
    pairs_out,
    x_out,
    cots_out,
    xs,
    raw_gate,
    raw_up,
    raw_down,
    w_gate,
    w_up,
    w_down,
    terms,
    half_a,
    full_a,
    sums,
    half_b,
    full_b,
    acts,
    hidden_t,
    pairs,
    x_t,
    cots,
    out_acc,
    gradx_acc,
    tail_out,
    tail_core,
    tables,
    slot_at,
    load_sem,
    save_sem,
    head_send,
    head_recv,
    send_sem,
    recv_sem,
    tail_send,
    tail_recv,
):
    row, col = lax.axis_index("row"), lax.axis_index("col")
    z, y = row // 4, row % 4
    ix, core = col // 2, col % 2

    def y_dev(step):
        return (z * 4 + (y + step) % 4, col)

    def z_dev(step):
        return (((z + step) % 4) * 4 + y, col)

    def x_dev(step):
        return (row, ((ix + step) % 4) * 2 + core)

    sibling = (row, ix * 2 + 1 - core)

    loads = [
        pltpu.make_async_copy(x_in, xs.at[col, 0], load_sem.at[0]),
        pltpu.make_async_copy(cot_in, xs.at[col, 1], load_sem.at[1]),
        pltpu.make_async_copy(gate_in, raw_gate.at[pl.ds(0, NB)], load_sem.at[2]),
        pltpu.make_async_copy(up_in, raw_up.at[pl.ds(0, NB)], load_sem.at[3]),
        pltpu.make_async_copy(down_in, raw_down.at[pl.ds(0, NB)], load_sem.at[4]),
    ]
    loads[0].start()
    loads[1].start()

    barrier = pltpu.get_barrier_semaphore()
    for dev in (y_dev(1), y_dev(3), z_dev(1), z_dev(3), x_dev(1), x_dev(3), sibling):
        pl.semaphore_signal(barrier, inc=1, device_id=dev, device_id_type=MESH)

    zero = jnp.zeros((BLOCK, BLOCK), BF16)
    raw_gate[NB] = zero
    raw_up[NB] = zero
    raw_down[NB] = zero
    out_acc[...] = jnp.zeros_like(out_acc)
    gradx_acc[...] = jnp.zeros_like(gradx_acc)

    pl.semaphore_wait(barrier, 7)

    def head(n, src, dst, dev):
        return pltpu.make_async_remote_copy(
            src_ref=src,
            dst_ref=dst,
            send_sem=head_send.at[0],
            recv_sem=head_recv.at[HEAD_SEM[n]],
            device_id=dev,
            device_id_type=MESH,
        )

    other = 1 - core
    right, left = x_dev(1), x_dev(3)

    def at_x(step, side, arr):
        return xs.at[((ix + step) % 4) * 2 + side, arr]

    def head_start(n, src, dst, dev):
        head(n, src, dst, dev).start()

    def forward(n, ref, dev):
        head_start(n, ref, ref, dev)

    def head_wait(n, ref):
        head(n, ref, ref, right).wait_recv()

    head_start(0, x_in, xs.at[col, 0], right)
    head_start(1, cot_in, xs.at[col, 1], left)
    head_start(2, cot_in, xs.at[col, 1], right)
    head_start(3, x_in, xs.at[col, 0], left)
    head_start(4, x_in, xs.at[col, 0], sibling)
    head_start(5, cot_in, xs.at[col, 1], sibling)
    for load in loads[2:]:
        load.start()

    spots = lax.broadcasted_iota(jnp.int32, (8, 128), 0) * 128 + lax.broadcasted_iota(
        jnp.int32, (8, 128), 1
    )

    def enter(n, both):
        gate_tab, down_tab = both
        gate_tab = jnp.where(spots == gate_slots[0, 0, n], n, gate_tab)
        down_tab = jnp.where(spots == down_slots[0, 0, n], n, down_tab)
        return gate_tab, down_tab

    nowhere = jnp.full((8, 128), NB, jnp.int32)
    gate_tab, down_tab = lax.fori_loop(0, NB, enter, (nowhere, nowhere), unroll=8)
    tables[0] = jnp.where(gate_tab < gate_count[0, 0], gate_tab, NB)
    tables[1] = jnp.where(down_tab < down_count[0, 0], down_tab, NB)
    to_scalars = pltpu.make_async_copy(tables, slot_at, load_sem.at[5])
    to_scalars.start()

    def find(table, spot):
        return slot_at[table, spot // 128, spot % 128]

    def place_gate(k, carry):
        for raw, dense in ((raw_gate, w_gate), (raw_up, w_up)):
            for r in range(DPB):
                for b in range(2):
                    slot = find(0, r * FPB + 2 * k + b)
                    dense[k, r * BLOCK : (r + 1) * BLOCK, b * BLOCK : (b + 1) * BLOCK] = raw[slot]
        return carry

    def place_down(k, carry):
        for r in range(DPB):
            for b in range(2):
                slot = find(1, r * FPB + 2 * k + b)
                w_down[k, b * BLOCK : (b + 1) * BLOCK, r * BLOCK : (r + 1) * BLOCK] = raw_down[slot]
        return carry

    to_scalars.wait()
    loads[2].wait()
    loads[3].wait()
    lax.fori_loop(0, 4, place_gate, 0)

    head_wait(0, at_x(3, core, 0))
    forward(6, at_x(3, core, 0), right)
    forward(7, at_x(3, core, 0), sibling)
    head_wait(1, at_x(1, core, 1))
    forward(8, at_x(1, core, 1), left)
    forward(9, at_x(1, core, 1), sibling)

    lax.fori_loop(4, 8, place_gate, 0)

    head_wait(2, at_x(3, core, 1))
    forward(10, at_x(3, core, 1), sibling)
    head_wait(3, at_x(1, core, 0))
    forward(11, at_x(1, core, 0), sibling)

    lax.fori_loop(8, CHUNKS, place_gate, 0)
    loads[4].wait()
    lax.fori_loop(0, 4, place_down, 0)

    head_wait(6, at_x(2, core, 0))
    forward(12, at_x(2, core, 0), sibling)
    head_wait(8, at_x(2, core, 1))
    forward(13, at_x(2, core, 1), sibling)

    lax.fori_loop(4, CHUNKS, place_down, 0)

    head_wait(4, xs.at[pl.ds(0, 4)])
    loads[0].wait()
    loads[1].wait()

    save_x = pltpu.make_async_copy(x_t, x_out, save_sem.at[0])
    save_cots = pltpu.make_async_copy(cots, cots_out, save_sem.at[1])

    def lay_out_inputs():
        for r in range(DPB):
            cols = slice(r * BLOCK, (r + 1) * BLOCK)
            x_t[r] = xs[:, 0, :, cols].reshape(TOKENS, BLOCK).T
            cots[r] = xs[:, 1, :, cols].reshape(TOKENS, BLOCK)
        save_x.start()
        save_cots.start()

    def places(k):
        odd = k % 2
        i = (1 - odd) * y + odd * z
        j = (1 - odd) * z + odd * y

        def dev(step, along_z):
            y_new = (y + (1 - along_z) * step) % 4
            z_new = (z + along_z * step) % 4
            return (z_new * 4 + y_new, col)

        return i, j, dev(1, odd), dev(3, odd), dev(1, 1 - odd), dev(3, 1 - odd)

    def swap(k, a, b):
        turned = k // (CHUNKS - 1)
        return (1 - turned) * a + turned * b, (1 - turned) * b + turned * a

    def gather_places(k):
        i, j, ar, al, br, bl = places(k)
        p, q = swap(k, i, j)
        pick = lambda a, b: tuple(swap(k, m, n)[0] for m, n in zip(a, b))
        return p, q, pick(ar, br), pick(al, bl), pick(br, ar), pick(bl, al)

    def copy(k, n, src, dst, dev):
        return pltpu.make_async_remote_copy(
            src_ref=src,
            dst_ref=dst,
            send_sem=send_sem.at[k, SEND_SEM[n]],
            recv_sem=recv_sem.at[k, RECV_SEM[n]],
            device_id=dev,
            device_id_type=MESH,
        )

    def all_copies(k):
        i, j, ar, al, br, bl = places(k)
        i1, i2, i3 = (i + 1) % 4, (i + 2) % 4, (i + 3) % 4
        j1, j2, j3 = (j + 1) % 4, (j + 2) % 4, (j + 3) % 4
        p, q, p_right, p_left, q_right, q_left = gather_places(k)
        p1, p3, q1, q3 = (p + 1) % 4, (p + 3) % 4, (q + 1) % 4, (q + 3) % 4
        same = lambda n, ref, dev: copy(k, n, ref, ref, dev)
        near, far = pl.ds(0, 2), pl.ds(2, 2)
        return [
            lambda: copy(k, 0, terms.at[k, i2, 0], half_a.at[k, 0], ar),
            lambda: copy(k, 1, terms.at[k, i2, 1], half_a.at[k, 1], al),
            lambda: copy(k, 2, terms.at[k, i1, 1], full_a.at[k, 0, 1], ar),
            lambda: copy(k, 3, terms.at[k, i3, 0], full_a.at[k, 1, 0], al),
            lambda: copy(k, 4, terms.at[k, i1, 0], full_a.at[k, 0, 0], ar),
            lambda: copy(k, 5, terms.at[k, i3, 1], full_a.at[k, 1, 1], al),
            lambda: copy(k, 6, sums.at[k, j2, 0], half_b.at[k, 0], br),
            lambda: copy(k, 7, sums.at[k, j2, 1], half_b.at[k, 1], bl),
            lambda: copy(k, 8, sums.at[k, j1], full_b.at[k, 0], br),
            lambda: copy(k, 9, sums.at[k, j3], full_b.at[k, 1], bl),
            lambda: same(10, acts.at[k, p, q], q_right),
            lambda: same(11, acts.at[k, p, q], q_left),
            lambda: same(12, acts.at[k, p, q3, 0], q_right),
            lambda: same(13, acts.at[k, p, q1, 1], q_left),
            lambda: same(14, acts.at[k, p, near], p_right),
            lambda: same(15, acts.at[k, p, far], p_left),
            lambda: same(16, acts.at[k, p, far], p_right),
            lambda: same(17, acts.at[k, p, near], p_left),
            lambda: same(18, acts.at[k, p3, near], p_right),
            lambda: same(19, acts.at[k, p1, far], p_left),
        ]

    def arrived(k, n, ref):
        i, j, ar, al, br, bl = places(k)
        copy(k, n, ref, ref, ar).wait_recv()

    def left_here(k, n, ref):
        i, j, ar, al, br, bl = places(k)
        copy(k, n, ref, ref, ar).wait_send()

    def plus(a, b):
        return (a.astype(F32) + b.astype(F32)).astype(BF16)

    def p0(k):
        for part, (arr, weights) in enumerate(((0, w_gate), (0, w_up), (1, w_down))):
            if part < 2:
                lhs = xs[:, 0].reshape(TOKENS, WIDTH)
                val = jnp.dot(lhs, weights[k], preferred_element_type=F32)
            else:
                lhs = xs[:, 1].reshape(TOKENS, WIDTH)
                val = nt_dot(lhs, weights[k])
            val = val.astype(BF16)
            for b in range(2):
                terms[k, :, b, :, part * 16 : (part + 1) * 16, :] = val[
                    :, b * BLOCK : (b + 1) * BLOCK
                ].reshape(4, 4, 16, BLOCK)
        copies = all_copies(k)
        for n in range(4):
            copies[n]().start()

    def p1(k):
        i, j, *_ = places(k)
        i1, i3 = (i + 1) % 4, (i + 3) % 4
        copies = all_copies(k)
        arrived(k, 0, half_a.at[k])
        terms[k, i1, 0] = plus(terms[k, i1, 0], half_a[k, 0])
        copies[4]().start()
        terms[k, i3, 1] = plus(terms[k, i3, 1], half_a[k, 1])
        copies[5]().start()

    def p2(k):
        i, j, *_ = places(k)
        copies = all_copies(k)
        arrived(k, 2, full_a.at[k])
        for b in range(2):
            total = terms[k, i, b].astype(F32) + full_a[k, 0, b].astype(F32)
            sums[k, :, b] = (total + full_a[k, 1, b].astype(F32)).astype(BF16)
        copies[6]().start()
        copies[7]().start()

    def p3(k):
        i, j, *_ = places(k)
        j1, j3 = (j + 1) % 4, (j + 3) % 4
        copies = all_copies(k)
        arrived(k, 6, half_b.at[k])
        sums[k, j1, 0] = plus(sums[k, j1, 0], half_b[k, 0])
        copies[8]().start()
        sums[k, j3, 1] = plus(sums[k, j3, 1], half_b[k, 1])
        copies[9]().start()

    def p4(k):
        i, j, *_ = places(k)
        p, q, *_ = gather_places(k)
        copies = all_copies(k)
        arrived(k, 8, full_b.at[k])
        total = sums[k, j].astype(F32) + full_b[k, 0].astype(F32) + full_b[k, 1].astype(F32)
        gate, up, grad = total[:, 0:16], total[:, 16:32], total[:, 32:48]
        sigma = 1.0 / (1.0 + jnp.exp(-gate))
        acts[k, p, q, :, 0:16, :] = (gate * sigma * up).astype(BF16)
        acts[k, p, q, :, 16:32, :] = (grad * up * sigma * (1.0 + gate * (1.0 - sigma))).astype(BF16)
        acts[k, p, q, :, 32:48, :] = (grad * gate * sigma).astype(BF16)
        copies[10]().start()
        copies[11]().start()

    def p5(k):
        p, q, *_ = gather_places(k)
        copies = all_copies(k)
        arrived(k, 10, acts.at[k, p, pl.ds(0, 2)])
        copies[12]().start()
        copies[13]().start()

    def p6(k):
        p, q, *_ = gather_places(k)
        copies = all_copies(k)
        arrived(k, 12, acts.at[k, p, 0])
        for n in range(14, 18):
            copies[n]().start()

    def p7(k):
        p, q, *_ = gather_places(k)
        copies = all_copies(k)
        arrived(k, 14, acts.at[k, 0])
        copies[18]().start()
        copies[19]().start()

    def saves(at):
        return (
            pltpu.make_async_copy(hidden_t.at[at], hidden_out.at[at], save_sem.at[2]),
            pltpu.make_async_copy(pairs.at[at], pairs_out.at[at], save_sem.at[3]),
        )

    def p8(k):
        p, q, *_ = gather_places(k)
        arrived(k, 16, acts.at[k, pl.ds(0, 2)])

        groups = [swap(k, a, b) for a in range(4) for b in range(4)]

        def act(part):
            cols = [
                jnp.concatenate([acts[k, u, v, b, part * 16 : (part + 1) * 16, :] for u, v in groups])
                for b in range(2)
            ]
            return cols, jnp.concatenate(cols, axis=1)

        (_, hidden), (gate_cols, grad_gate), (up_cols, grad_up) = act(0), act(1), act(2)
        for n in range(4):
            cols = slice(n * 256, (n + 1) * 256)
            out = jnp.dot(hidden, w_down[k, :, cols], preferred_element_type=F32)
            out_acc[:, :, cols] += out.reshape(8, 32, 256)
            grad = nt_dot(grad_gate, w_gate[k, cols, :]) + nt_dot(grad_up, w_up[k, cols, :])
            gradx_acc[:, :, cols] += grad.reshape(8, 32, 256)
        hidden_t[k] = hidden.T
        for b in range(2):
            pairs[k, b, :, 0:BLOCK] = gate_cols[b]
            pairs[k, b, :, BLOCK:] = up_cols[b]
        for save in saves(k):
            save.start()
        left_here(k, 0, terms.at[k, pl.ds(0, 3)])
        left_here(k, 6, terms.at[k, pl.ds(0, 3), 0])
        left_here(k, 14, terms.at[k, pl.ds(0, 3)])

    def tick(t, carry):
        for phase, late in zip((p7, p6, p5, p4, p3, p2, p1, p0, p8), LAGS[7::-1] + LAGS[8:]):
            k = t - late

            @pl.when(jnp.logical_and(k >= 0, k < CHUNKS))
            def _():
                phase(k)

        @pl.when(t == 6)
        def _():
            lay_out_inputs()

        return carry

    lax.fori_loop(0, CHUNKS + LAGS[8], tick, 0)

    def last(n, src, dst, dev):
        return pltpu.make_async_remote_copy(
            src_ref=src,
            dst_ref=dst,
            send_sem=tail_send.at[0],
            recv_sem=tail_recv.at[n],
            device_id=dev,
            device_id_type=MESH,
        )

    x0, x1, x2, x3 = ix, (ix + 1) % 4, (ix + 2) % 4, (ix + 3) % 4
    totals = (out_acc, gradx_acc)
    cores = {}
    for n, at in ((0, x2), (1, x1), (2, x3), (3, x0)):
        for arr in range(2):
            tail_out[at, arr] = totals[arr][at * 2 + other].astype(BF16)
        cores[n] = last(n, tail_out.at[at], tail_core.at[at], sibling)
        cores[n].start()

    for n, at, ref in ((0, x2, part2_ref), (1, x1, part1_ref), (2, x3, part3_ref), (3, x0, mine_ref)):
        cores[n].wait_recv()
        for arr in range(2):
            mine = totals[arr][at * 2 + core] + tail_core[at, arr].astype(F32)
            ref[arr] = mine.astype(ref.dtype)

    last(0, tail_out, tail_core, sibling).wait_send()
    head(0, xs.at[pl.ds(0, 7)], xs.at[pl.ds(0, 7)], right).wait_send()
    save_x.wait()
    save_cots.wait()

    for save in saves(pl.ds(0, CHUNKS)):
        save.wait()


def run_layer(gate_slots, gate_count, down_slots, down_count, inputs, grad_out, gate_blocks, up_blocks, down_blocks):
    anywhere = pl.BlockSpec(memory_space=pl.ANY)
    scalars = pl.BlockSpec(memory_space=pltpu.SMEM)
    vmem = pl.BlockSpec(memory_space=pltpu.VMEM)
    raw = pltpu.VMEM((NB + 1, BLOCK, BLOCK), BF16)
    part = (48, BLOCK)
    part_of_sum = jax.ShapeDtypeStruct((2, 32, WIDTH), BF16)
    return pl.pallas_call(
        layer_kernel,
        out_shape=(
            part_of_sum,
            part_of_sum,
            part_of_sum,
            jax.ShapeDtypeStruct((2, 32, WIDTH), F32),
            jax.ShapeDtypeStruct((CHUNKS, CHUNK, TOKENS), BF16),
            jax.ShapeDtypeStruct((CHUNKS, 2, TOKENS, 2 * BLOCK), BF16),
            jax.ShapeDtypeStruct((DPB, BLOCK, TOKENS), BF16),
            jax.ShapeDtypeStruct((DPB, TOKENS, BLOCK), BF16),
        ),
        in_specs=[scalars] * 4 + [anywhere] * 5,
        out_specs=(vmem,) * 4 + (anywhere,) * 4,
        scratch_shapes=[
            pltpu.VMEM((8, 2, 32, WIDTH), BF16),
            raw,
            raw,
            raw,
            pltpu.VMEM((CHUNKS, WIDTH, CHUNK), BF16),
            pltpu.VMEM((CHUNKS, WIDTH, CHUNK), BF16),
            pltpu.VMEM((CHUNKS, CHUNK, WIDTH), BF16),
            pltpu.VMEM((CHUNKS, 4, 2, 4) + part, BF16),
            pltpu.VMEM((CHUNKS, 2, 4) + part, BF16),
            pltpu.VMEM((CHUNKS, 2, 2, 4) + part, BF16),
            pltpu.VMEM((CHUNKS, 4, 2) + part, BF16),
            pltpu.VMEM((CHUNKS, 2) + part, BF16),
            pltpu.VMEM((CHUNKS, 2, 2) + part, BF16),
            pltpu.VMEM((CHUNKS, 4, 4, 2) + part, BF16),
            pltpu.VMEM((CHUNKS, CHUNK, TOKENS), BF16),
            pltpu.VMEM((CHUNKS, 2, TOKENS, 2 * BLOCK), BF16),
            pltpu.VMEM((DPB, BLOCK, TOKENS), BF16),
            pltpu.VMEM((DPB, TOKENS, BLOCK), BF16),
            pltpu.VMEM((8, 32, WIDTH), F32),
            pltpu.VMEM((8, 32, WIDTH), F32),
            pltpu.VMEM((4, 2, 32, WIDTH), BF16),
            pltpu.VMEM((4, 2, 32, WIDTH), BF16),
            pltpu.VMEM((2, 8, 128), jnp.int32),
            pltpu.SMEM((2, 8, 128), jnp.int32),
            pltpu.SemaphoreType.DMA((6,)),
            pltpu.SemaphoreType.DMA((4,)),
            pltpu.SemaphoreType.DMA((1,)),
            pltpu.SemaphoreType.DMA((7,)),
            pltpu.SemaphoreType.DMA((CHUNKS, 3)),
            pltpu.SemaphoreType.DMA((CHUNKS, 8)),
            pltpu.SemaphoreType.DMA((1,)),
            pltpu.SemaphoreType.DMA((4,)),
        ],
        compiler_params=pltpu.CompilerParams(
            collective_id=0, has_side_effects=True, vmem_limit_bytes=60 * 2**20
        ),
        name="layer",
    )(gate_slots, gate_count, down_slots, down_count, inputs, grad_out, gate_blocks, up_blocks, down_blocks)


def grads_kernel(
    gate_slots,
    gate_count,
    down_slots,
    down_count,
    hidden_in,
    pairs_in,
    x_in,
    cots_in,
    gate_out,
    up_out,
    down_out,
    hidden_t,
    pairs,
    x_t,
    cots,
    gate_stage,
    up_stage,
    down_stage,
    load_sem,
    save_sem,
):
    loads = [
        pltpu.make_async_copy(cots_in, cots, load_sem.at[0]),
        pltpu.make_async_copy(hidden_in, hidden_t, load_sem.at[1]),
        pltpu.make_async_copy(x_in, x_t, load_sem.at[2]),
        pltpu.make_async_copy(pairs_in, pairs, load_sem.at[3]),
    ]
    for load in loads:
        load.start()
    groups = NB // GROUP

    def save(kind, stage, out, g):
        rows = pl.ds(g * GROUP, GROUP)
        return pltpu.make_async_copy(stage.at[rows], out.at[rows], save_sem.at[kind, g])

    loads[0].wait()
    loads[1].wait()

    def down_group(g, carry):
        first = g * GROUP
        live = down_count[0, 0] - first

        @pl.when(live > 0)
        def _():
            for u in range(GROUP):
                spot = down_slots[0, 0, first + u]
                val = jnp.dot(hidden_t[spot % FPB], cots[spot // FPB], preferred_element_type=F32)
                down_stage[first + u] = jnp.where(u < live, val, 0.0).astype(BF16)

        @pl.when(live <= 0)
        def _():
            down_stage[pl.ds(first, GROUP)] = jnp.zeros((GROUP, BLOCK, BLOCK), BF16)

        save(0, down_stage, down_out, g).start()
        return carry

    lax.fori_loop(0, groups, down_group, 0)
    loads[2].wait()
    loads[3].wait()

    def gate_group(g, carry):
        first = g * GROUP
        live = gate_count[0, 0] - first

        @pl.when(live > 0)
        def _():
            for u in range(GROUP):
                spot = gate_slots[0, 0, first + u]
                val = jnp.dot(x_t[spot // FPB], pairs[spot % FPB], preferred_element_type=F32)
                val = jnp.where(u < live, val, 0.0).astype(BF16)
                gate_stage[first + u] = val[:, 0:BLOCK]
                up_stage[first + u] = val[:, BLOCK:]

        @pl.when(live <= 0)
        def _():
            zero = jnp.zeros((GROUP, BLOCK, BLOCK), BF16)
            gate_stage[pl.ds(first, GROUP)] = zero
            up_stage[pl.ds(first, GROUP)] = zero

        save(1, gate_stage, gate_out, g).start()
        save(2, up_stage, up_out, g).start()
        return carry

    lax.fori_loop(0, groups, gate_group, 0)

    def finish(g, carry):
        save(0, down_stage, down_out, g).wait()
        save(1, gate_stage, gate_out, g).wait()
        save(2, up_stage, up_out, g).wait()
        return carry

    lax.fori_loop(0, groups, finish, 0)


def run_grads(gate_slots, gate_count, down_slots, down_count, hidden, pairs, x_t, cots):
    scalars = pl.BlockSpec(memory_space=pltpu.SMEM)
    anywhere = pl.BlockSpec(memory_space=pl.ANY)
    grads = jax.ShapeDtypeStruct((NB, BLOCK, BLOCK), BF16)
    return pl.pallas_call(
        grads_kernel,
        out_shape=(grads, grads, grads),
        in_specs=[scalars] * 4 + [anywhere] * 4,
        out_specs=(anywhere, anywhere, anywhere),
        scratch_shapes=[
            pltpu.VMEM((FPB, BLOCK, TOKENS), BF16),
            pltpu.VMEM((FPB, TOKENS, 2 * BLOCK), BF16),
            pltpu.VMEM((DPB, BLOCK, TOKENS), BF16),
            pltpu.VMEM((DPB, TOKENS, BLOCK), BF16),
            pltpu.VMEM((NB, BLOCK, BLOCK), BF16),
            pltpu.VMEM((NB, BLOCK, BLOCK), BF16),
            pltpu.VMEM((NB, BLOCK, BLOCK), BF16),
            pltpu.SemaphoreType.DMA((4,)),
            pltpu.SemaphoreType.DMA((3, NB // GROUP)),
        ],
        compiler_params=pltpu.CompilerParams(vmem_limit_bytes=60 * 2**20),
        cost_estimate=pl.CostEstimate(
            flops=6 * NB * BLOCK * BLOCK * TOKENS, bytes_accessed=32 * 2**20, transcendentals=0
        ),
        name="block_grads",
    )(gate_slots, gate_count, down_slots, down_count, hidden, pairs, x_t, cots)


def to_plane(value, step):
    cols = lax.axis_size("col")
    return lax.ppermute(value, "col", [(c, (c + 2 * step) % cols) for c in range(cols)])


def local(
    inputs,
    grad_out,
    gate_blocks,
    up_blocks,
    down_blocks,
    gate_slots,
    gate_count,
    down_slots,
    down_count,
):
    part1, part2, part3, mine, hidden, pairs, x_t, cots = run_layer(
        gate_slots,
        gate_count,
        down_slots,
        down_count,
        inputs,
        grad_out,
        gate_blocks[0, 0],
        up_blocks[0, 0],
        down_blocks[0, 0],
    )
    arrived = [to_plane(part2, 2), to_plane(part1, 1), to_plane(part3, 3)]
    hidden = hidden.reshape(FPB, BLOCK, TOKENS)
    pairs = pairs.reshape(FPB, TOKENS, 2 * BLOCK)
    grads = run_grads(gate_slots, gate_count, down_slots, down_count, hidden, pairs, x_t, cots)
    total = mine + sum(part.astype(F32) for part in arrived)
    layer_out, grad_x = total[0].astype(BF16), total[1].astype(BF16)
    return (layer_out, grad_x) + tuple(grad[None, None] for grad in grads)


def solution(mesh):
    tokens = P("col", "row")
    blocks = P("row", "col", None, None, None)
    slots = P("row", "col", None)
    count = P("row", "col")
    return jax.shard_map(
        local,
        mesh=mesh,
        in_specs=(tokens, tokens, blocks, blocks, blocks, slots, count, slots, count),
        out_specs=(tokens, tokens, blocks, blocks, blocks),
        check_vma=False,
    )
```

```python
import jax
import jax.numpy as jnp
from jax import lax
from jax.experimental import pallas as pl
from jax.experimental.pallas import tpu as pltpu
from jax.sharding import PartitionSpec as P

TOKENS = 256
BLOCK = 128
NB = 96
DPB = 8
FPB = 26
WIDTH = DPB * BLOCK
CHUNK = 2 * BLOCK
CHUNKS = FPB // 2
GROUP = 16
LAGS = (0, 4, 8, 12, 16, 20, 24, 28, 32)
MESH = pl.DeviceIdType.MESH
TAIL_SEND = (0,) * 4 + (1,) * 6
TAIL_RECV = (0, 1, 2, 3, 4, 5) + (6,) * 4
HEAD_SEM = (0, 1, 2, 3, 6, 6, 4, 6, 5, 6, 6, 6, 6, 6)
SEND_SEM = (0,) * 6 + (1,) * 8 + (2,) * 6
RECV_SEM = (0, 0, 1, 1, 1, 1, 2, 2, 3, 3, 4, 4, 5, 5, 6, 6, 7, 7, 7, 7)
F32 = jnp.float32
BF16 = jnp.bfloat16


def nt_dot(a, b):
    return lax.dot_general(a, b, (((1,), (1,)), ((), ())), preferred_element_type=F32)


def layer_kernel(
    gate_slots,
    gate_count,
    down_slots,
    down_count,
    x_in,
    cot_in,
    gate_in,
    up_in,
    down_in,
    layer_ref,
    raw_gate,
    raw_up,
    raw_down,
    xs,
    w_gate,
    w_up,
    w_down,
    terms,
    half_a,
    full_a,
    sums,
    half_b,
    full_b,
    acts,
    hidden_t,
    pairs,
    x_t,
    cots,
    out_acc,
    gradx_acc,
    tail_out,
    tail,
    tail_core,
    tail_h,
    tail_f,
    tables,
    slot_at,
    load_sem,
    head_send,
    head_recv,
    send_sem,
    recv_sem,
    tail_send,
    tail_recv,
):
    row, col = lax.axis_index("row"), lax.axis_index("col")
    z, y = row // 4, row % 4
    ix, core = col // 2, col % 2

    def y_dev(step):
        return (z * 4 + (y + step) % 4, col)

    def z_dev(step):
        return (((z + step) % 4) * 4 + y, col)

    def x_dev(step):
        return (row, ((ix + step) % 4) * 2 + core)

    sibling = (row, ix * 2 + 1 - core)

    loads = [
        pltpu.make_async_copy(x_in, xs.at[col, 0], load_sem.at[0]),
        pltpu.make_async_copy(cot_in, xs.at[col, 1], load_sem.at[1]),
        pltpu.make_async_copy(gate_in, raw_gate.at[pl.ds(0, NB)], load_sem.at[2]),
        pltpu.make_async_copy(up_in, raw_up.at[pl.ds(0, NB)], load_sem.at[3]),
        pltpu.make_async_copy(down_in, raw_down.at[pl.ds(0, NB)], load_sem.at[4]),
    ]
    loads[0].start()
    loads[1].start()

    barrier = pltpu.get_barrier_semaphore()
    for dev in (y_dev(1), y_dev(3), z_dev(1), z_dev(3), x_dev(1), x_dev(3), sibling):
        pl.semaphore_signal(barrier, inc=1, device_id=dev, device_id_type=MESH)

    zero = jnp.zeros((BLOCK, BLOCK), BF16)
    raw_gate[NB] = zero
    raw_up[NB] = zero
    raw_down[NB] = zero
    out_acc[...] = jnp.zeros_like(out_acc)
    gradx_acc[...] = jnp.zeros_like(gradx_acc)

    pl.semaphore_wait(barrier, 7)

    def head(n, src, dst, dev):
        return pltpu.make_async_remote_copy(
            src_ref=src,
            dst_ref=dst,
            send_sem=head_send.at[0],
            recv_sem=head_recv.at[HEAD_SEM[n]],
            device_id=dev,
            device_id_type=MESH,
        )

    other = 1 - core
    right, left = x_dev(1), x_dev(3)

    def at_x(step, side, arr):
        return xs.at[((ix + step) % 4) * 2 + side, arr]

    def head_start(n, src, dst, dev):
        head(n, src, dst, dev).start()

    def forward(n, ref, dev):
        head_start(n, ref, ref, dev)

    def head_wait(n, ref):
        head(n, ref, ref, right).wait_recv()

    head_start(0, x_in, xs.at[col, 0], right)
    head_start(1, cot_in, xs.at[col, 1], left)
    head_start(2, cot_in, xs.at[col, 1], right)
    head_start(3, x_in, xs.at[col, 0], left)
    head_start(4, x_in, xs.at[col, 0], sibling)
    head_start(5, cot_in, xs.at[col, 1], sibling)
    for load in loads[2:]:
        load.start()

    spots = lax.broadcasted_iota(jnp.int32, (8, 128), 0) * 128 + lax.broadcasted_iota(
        jnp.int32, (8, 128), 1
    )

    def enter(n, both):
        gate_tab, down_tab = both
        gate_tab = jnp.where(spots == gate_slots[0, 0, n], n, gate_tab)
        down_tab = jnp.where(spots == down_slots[0, 0, n], n, down_tab)
        return gate_tab, down_tab

    nowhere = jnp.full((8, 128), NB, jnp.int32)
    gate_tab, down_tab = lax.fori_loop(0, NB, enter, (nowhere, nowhere), unroll=8)
    tables[0] = jnp.where(gate_tab < gate_count[0, 0], gate_tab, NB)
    tables[1] = jnp.where(down_tab < down_count[0, 0], down_tab, NB)
    to_scalars = pltpu.make_async_copy(tables, slot_at, load_sem.at[5])
    to_scalars.start()

    def find(table, spot):
        return slot_at[table, spot // 128, spot % 128]

    def place_gate(k, carry):
        for raw, dense in ((raw_gate, w_gate), (raw_up, w_up)):
            for r in range(DPB):
                for b in range(2):
                    slot = find(0, r * FPB + 2 * k + b)
                    dense[k, r * BLOCK : (r + 1) * BLOCK, b * BLOCK : (b + 1) * BLOCK] = raw[slot]
        return carry

    def place_down(k, carry):
        for r in range(DPB):
            for b in range(2):
                slot = find(1, r * FPB + 2 * k + b)
                w_down[k, b * BLOCK : (b + 1) * BLOCK, r * BLOCK : (r + 1) * BLOCK] = raw_down[slot]
        return carry

    to_scalars.wait()
    loads[2].wait()
    loads[3].wait()
    lax.fori_loop(0, 4, place_gate, 0)

    head_wait(0, at_x(3, core, 0))
    forward(6, at_x(3, core, 0), right)
    forward(7, at_x(3, core, 0), sibling)
    head_wait(1, at_x(1, core, 1))
    forward(8, at_x(1, core, 1), left)
    forward(9, at_x(1, core, 1), sibling)

    lax.fori_loop(4, 8, place_gate, 0)

    head_wait(2, at_x(3, core, 1))
    forward(10, at_x(3, core, 1), sibling)
    head_wait(3, at_x(1, core, 0))
    forward(11, at_x(1, core, 0), sibling)

    lax.fori_loop(8, CHUNKS, place_gate, 0)
    loads[4].wait()
    lax.fori_loop(0, 4, place_down, 0)

    head_wait(6, at_x(2, core, 0))
    forward(12, at_x(2, core, 0), sibling)
    head_wait(8, at_x(2, core, 1))
    forward(13, at_x(2, core, 1), sibling)

    lax.fori_loop(4, CHUNKS, place_down, 0)

    head_wait(4, xs.at[pl.ds(0, 4)])
    loads[0].wait()
    loads[1].wait()

    def lay_out_inputs():
        for r in range(DPB):
            cols = slice(r * BLOCK, (r + 1) * BLOCK)
            x_t[r] = xs[:, 0, :, cols].reshape(TOKENS, BLOCK).T
            cots[r] = xs[:, 1, :, cols].reshape(TOKENS, BLOCK)

    def places(k):
        odd = k % 2
        i = (1 - odd) * y + odd * z
        j = (1 - odd) * z + odd * y

        def dev(step, along_z):
            y_new = (y + (1 - along_z) * step) % 4
            z_new = (z + along_z * step) % 4
            return (z_new * 4 + y_new, col)

        return i, j, dev(1, odd), dev(3, odd), dev(1, 1 - odd), dev(3, 1 - odd)

    def swap(k, a, b):
        turned = k // (CHUNKS - 1)
        return (1 - turned) * a + turned * b, (1 - turned) * b + turned * a

    def gather_places(k):
        i, j, ar, al, br, bl = places(k)
        p, q = swap(k, i, j)
        pick = lambda a, b: tuple(swap(k, m, n)[0] for m, n in zip(a, b))
        return p, q, pick(ar, br), pick(al, bl), pick(br, ar), pick(bl, al)

    def copy(k, n, src, dst, dev):
        return pltpu.make_async_remote_copy(
            src_ref=src,
            dst_ref=dst,
            send_sem=send_sem.at[k, SEND_SEM[n]],
            recv_sem=recv_sem.at[k, RECV_SEM[n]],
            device_id=dev,
            device_id_type=MESH,
        )

    def all_copies(k):
        i, j, ar, al, br, bl = places(k)
        i1, i2, i3 = (i + 1) % 4, (i + 2) % 4, (i + 3) % 4
        j1, j2, j3 = (j + 1) % 4, (j + 2) % 4, (j + 3) % 4
        p, q, p_right, p_left, q_right, q_left = gather_places(k)
        p1, p3, q1, q3 = (p + 1) % 4, (p + 3) % 4, (q + 1) % 4, (q + 3) % 4
        same = lambda n, ref, dev: copy(k, n, ref, ref, dev)
        near, far = pl.ds(0, 2), pl.ds(2, 2)
        return [
            lambda: copy(k, 0, terms.at[k, i2, 0], half_a.at[k, 0], ar),
            lambda: copy(k, 1, terms.at[k, i2, 1], half_a.at[k, 1], al),
            lambda: copy(k, 2, terms.at[k, i1, 1], full_a.at[k, 0, 1], ar),
            lambda: copy(k, 3, terms.at[k, i3, 0], full_a.at[k, 1, 0], al),
            lambda: copy(k, 4, terms.at[k, i1, 0], full_a.at[k, 0, 0], ar),
            lambda: copy(k, 5, terms.at[k, i3, 1], full_a.at[k, 1, 1], al),
            lambda: copy(k, 6, sums.at[k, j2, 0], half_b.at[k, 0], br),
            lambda: copy(k, 7, sums.at[k, j2, 1], half_b.at[k, 1], bl),
            lambda: copy(k, 8, sums.at[k, j1], full_b.at[k, 0], br),
            lambda: copy(k, 9, sums.at[k, j3], full_b.at[k, 1], bl),
            lambda: same(10, acts.at[k, p, q], q_right),
            lambda: same(11, acts.at[k, p, q], q_left),
            lambda: same(12, acts.at[k, p, q3, 0], q_right),
            lambda: same(13, acts.at[k, p, q1, 1], q_left),
            lambda: same(14, acts.at[k, p, near], p_right),
            lambda: same(15, acts.at[k, p, far], p_left),
            lambda: same(16, acts.at[k, p, far], p_right),
            lambda: same(17, acts.at[k, p, near], p_left),
            lambda: same(18, acts.at[k, p3, near], p_right),
            lambda: same(19, acts.at[k, p1, far], p_left),
        ]

    def arrived(k, n, ref):
        i, j, ar, al, br, bl = places(k)
        copy(k, n, ref, ref, ar).wait_recv()

    def left_here(k, n, ref):
        i, j, ar, al, br, bl = places(k)
        copy(k, n, ref, ref, ar).wait_send()

    def plus(a, b):
        return (a.astype(F32) + b.astype(F32)).astype(BF16)

    def p0(k):
        for part, (arr, weights) in enumerate(((0, w_gate), (0, w_up), (1, w_down))):
            if part < 2:
                lhs = xs[:, 0].reshape(TOKENS, WIDTH)
                val = jnp.dot(lhs, weights[k], preferred_element_type=F32)
            else:
                lhs = xs[:, 1].reshape(TOKENS, WIDTH)
                val = nt_dot(lhs, weights[k])
            val = val.astype(BF16)
            for b in range(2):
                terms[k, :, b, :, part * 16 : (part + 1) * 16, :] = val[
                    :, b * BLOCK : (b + 1) * BLOCK
                ].reshape(4, 4, 16, BLOCK)
        copies = all_copies(k)
        for n in range(4):
            copies[n]().start()

    def p1(k):
        i, j, *_ = places(k)
        i1, i3 = (i + 1) % 4, (i + 3) % 4
        copies = all_copies(k)
        arrived(k, 0, half_a.at[k])
        terms[k, i1, 0] = plus(terms[k, i1, 0], half_a[k, 0])
        copies[4]().start()
        terms[k, i3, 1] = plus(terms[k, i3, 1], half_a[k, 1])
        copies[5]().start()

    def p2(k):
        i, j, *_ = places(k)
        copies = all_copies(k)
        arrived(k, 2, full_a.at[k])
        for b in range(2):
            total = terms[k, i, b].astype(F32) + full_a[k, 0, b].astype(F32)
            sums[k, :, b] = (total + full_a[k, 1, b].astype(F32)).astype(BF16)
        copies[6]().start()
        copies[7]().start()

    def p3(k):
        i, j, *_ = places(k)
        j1, j3 = (j + 1) % 4, (j + 3) % 4
        copies = all_copies(k)
        arrived(k, 6, half_b.at[k])
        sums[k, j1, 0] = plus(sums[k, j1, 0], half_b[k, 0])
        copies[8]().start()
        sums[k, j3, 1] = plus(sums[k, j3, 1], half_b[k, 1])
        copies[9]().start()

    def p4(k):
        i, j, *_ = places(k)
        p, q, *_ = gather_places(k)
        copies = all_copies(k)
        arrived(k, 8, full_b.at[k])
        total = sums[k, j].astype(F32) + full_b[k, 0].astype(F32) + full_b[k, 1].astype(F32)
        gate, up, grad = total[:, 0:16], total[:, 16:32], total[:, 32:48]
        sigma = 1.0 / (1.0 + jnp.exp(-gate))
        acts[k, p, q, :, 0:16, :] = (gate * sigma * up).astype(BF16)
        acts[k, p, q, :, 16:32, :] = (grad * up * sigma * (1.0 + gate * (1.0 - sigma))).astype(BF16)
        acts[k, p, q, :, 32:48, :] = (grad * gate * sigma).astype(BF16)
        copies[10]().start()
        copies[11]().start()

    def p5(k):
        p, q, *_ = gather_places(k)
        copies = all_copies(k)
        arrived(k, 10, acts.at[k, p, pl.ds(0, 2)])
        copies[12]().start()
        copies[13]().start()

    def p6(k):
        p, q, *_ = gather_places(k)
        copies = all_copies(k)
        arrived(k, 12, acts.at[k, p, 0])
        for n in range(14, 18):
            copies[n]().start()

    def p7(k):
        p, q, *_ = gather_places(k)
        copies = all_copies(k)
        arrived(k, 14, acts.at[k, 0])
        copies[18]().start()
        copies[19]().start()

    def p8(k):
        p, q, *_ = gather_places(k)
        arrived(k, 16, acts.at[k, pl.ds(0, 2)])

        groups = [swap(k, a, b) for a in range(4) for b in range(4)]

        def act(part):
            cols = [
                jnp.concatenate([acts[k, u, v, b, part * 16 : (part + 1) * 16, :] for u, v in groups])
                for b in range(2)
            ]
            return cols, jnp.concatenate(cols, axis=1)

        (_, hidden), (gate_cols, grad_gate), (up_cols, grad_up) = act(0), act(1), act(2)
        for n in range(4):
            cols = slice(n * 256, (n + 1) * 256)
            out = jnp.dot(hidden, w_down[k, :, cols], preferred_element_type=F32)
            out_acc[:, :, cols] += out.reshape(8, 32, 256)
            grad = nt_dot(grad_gate, w_gate[k, cols, :]) + nt_dot(grad_up, w_up[k, cols, :])
            gradx_acc[:, :, cols] += grad.reshape(8, 32, 256)
        hidden_t[pl.ds(2 * k, 2)] = hidden.T.reshape(2, BLOCK, TOKENS)
        for b in range(2):
            pairs[2 * k + b, :, 0:BLOCK] = gate_cols[b]
            pairs[2 * k + b, :, BLOCK:] = up_cols[b]
        left_here(k, 0, terms.at[k, pl.ds(0, 3)])
        left_here(k, 6, terms.at[k, pl.ds(0, 3), 0])
        left_here(k, 14, terms.at[k, pl.ds(0, 3)])

    def tick(t, carry):
        for phase, late in zip((p7, p6, p5, p4, p3, p2, p1, p0, p8), LAGS[7::-1] + LAGS[8:]):
            k = t - late

            @pl.when(jnp.logical_and(k >= 0, k < CHUNKS))
            def _():
                phase(k)

        @pl.when(t == 6)
        def _():
            lay_out_inputs()

        return carry

    lax.fori_loop(0, CHUNKS + LAGS[8], tick, 0)

    def down_group(g, carry):
        for u in range(GROUP):
            n = g * GROUP + u
            spot = down_slots[0, 0, n]
            val = jnp.dot(hidden_t[spot % FPB], cots[spot // FPB], preferred_element_type=F32)
            raw_down[n] = jnp.where(n < down_count[0, 0], val, 0.0).astype(BF16)
        return carry

    def gate_group(g, carry):
        for u in range(GROUP):
            n = g * GROUP + u
            spot = gate_slots[0, 0, n]
            val = jnp.dot(x_t[spot // FPB], pairs[spot % FPB], preferred_element_type=F32)
            val = jnp.where(n < gate_count[0, 0], val, 0.0).astype(BF16)
            raw_gate[n] = val[:, 0:BLOCK]
            raw_up[n] = val[:, BLOCK:]
        return carry

    def last(n, src, dst, dev):
        return pltpu.make_async_remote_copy(
            src_ref=src,
            dst_ref=dst,
            send_sem=tail_send.at[TAIL_SEND[n]],
            recv_sem=tail_recv.at[TAIL_RECV[n]],
            device_id=dev,
            device_id_type=MESH,
        )

    x0, x1, x2, x3 = ix, (ix + 1) % 4, (ix + 2) % 4, (ix + 3) % 4
    totals = (out_acc, gradx_acc)
    cores = {}
    for n, at in ((0, x2), (1, x1), (2, x3), (3, x0)):
        for arr in range(2):
            tail_out[at, arr] = totals[arr][at * 2 + other].astype(BF16)
        cores[n] = last(n, tail_out.at[at], tail_core.at[at], sibling)
        cores[n].start()

    def both(n, at):
        cores[n].wait_recv()
        for arr in range(2):
            mine = totals[arr][at * 2 + core] + tail_core[at, arr].astype(F32)
            tail[at, arr] = mine.astype(BF16)

    steps = [
        last(4, tail.at[x2, 0], tail_h.at[0], right),
        last(5, tail.at[x2, 1], tail_h.at[1], left),
        last(6, tail.at[x1, 1], tail_f.at[0, 1], right),
        last(7, tail.at[x3, 0], tail_f.at[1, 0], left),
        last(8, tail.at[x1, 0], tail_f.at[0, 0], right),
        last(9, tail.at[x3, 1], tail_f.at[1, 1], left),
    ]
    lax.fori_loop(0, 2, down_group, 0)
    both(0, x2)
    steps[0].start()
    steps[1].start()
    both(1, x1)
    steps[2].start()
    both(2, x3)
    steps[3].start()
    lax.fori_loop(2, 6, down_group, 0)
    lax.fori_loop(0, 3, gate_group, 0)
    steps[0].wait_recv()
    tail[x1, 0] = plus(tail[x1, 0], tail_h[0])
    steps[4].start()
    steps[1].wait_recv()
    tail[x3, 1] = plus(tail[x3, 1], tail_h[1])
    steps[5].start()
    lax.fori_loop(3, 6, gate_group, 0)
    cores[3].wait_recv()
    last(6, tail_f, tail_f, right).wait_recv()
    for arr in range(2):
        total = totals[arr][x0 * 2 + core] + tail_core[x0, arr].astype(F32)
        total = total + tail_f[0, arr].astype(F32) + tail_f[1, arr].astype(F32)
        layer_ref[arr] = total.astype(BF16)

    last(0, tail_out, tail_core, sibling).wait_send()
    last(4, tail.at[pl.ds(0, 3)], tail.at[pl.ds(0, 3)], right).wait_send()
    head(0, xs.at[pl.ds(0, 7)], xs.at[pl.ds(0, 7)], right).wait_send()


def run_layer(gate_slots, gate_count, down_slots, down_count, inputs, grad_out, gate_blocks, up_blocks, down_blocks):
    anywhere = pl.BlockSpec(memory_space=pl.ANY)
    scalars = pl.BlockSpec(memory_space=pltpu.SMEM)
    vmem = pl.BlockSpec(memory_space=pltpu.VMEM)
    raw = pltpu.VMEM((NB + 1, BLOCK, BLOCK), BF16)
    part = (48, BLOCK)
    return pl.pallas_call(
        layer_kernel,
        out_shape=(
            pltpu.VMEM((2, 32, WIDTH), BF16),
            raw,
            raw,
            raw,
        ),
        in_specs=[scalars] * 4 + [anywhere] * 5,
        out_specs=(vmem,) * 4,
        scratch_shapes=[
            pltpu.VMEM((8, 2, 32, WIDTH), BF16),
            pltpu.VMEM((CHUNKS, WIDTH, CHUNK), BF16),
            pltpu.VMEM((CHUNKS, WIDTH, CHUNK), BF16),
            pltpu.VMEM((CHUNKS, CHUNK, WIDTH), BF16),
            pltpu.VMEM((CHUNKS, 4, 2, 4) + part, BF16),
            pltpu.VMEM((CHUNKS, 2, 4) + part, BF16),
            pltpu.VMEM((CHUNKS, 2, 2, 4) + part, BF16),
            pltpu.VMEM((CHUNKS, 4, 2) + part, BF16),
            pltpu.VMEM((CHUNKS, 2) + part, BF16),
            pltpu.VMEM((CHUNKS, 2, 2) + part, BF16),
            pltpu.VMEM((CHUNKS, 4, 4, 2) + part, BF16),
            pltpu.VMEM((FPB, BLOCK, TOKENS), BF16),
            pltpu.VMEM((FPB, TOKENS, 2 * BLOCK), BF16),
            pltpu.VMEM((DPB, BLOCK, TOKENS), BF16),
            pltpu.VMEM((DPB, TOKENS, BLOCK), BF16),
            pltpu.VMEM((8, 32, WIDTH), F32),
            pltpu.VMEM((8, 32, WIDTH), F32),
            pltpu.VMEM((4, 2, 32, WIDTH), BF16),
            pltpu.VMEM((4, 2, 32, WIDTH), BF16),
            pltpu.VMEM((4, 2, 32, WIDTH), BF16),
            pltpu.VMEM((2, 32, WIDTH), BF16),
            pltpu.VMEM((2, 2, 32, WIDTH), BF16),
            pltpu.VMEM((2, 8, 128), jnp.int32),
            pltpu.SMEM((2, 8, 128), jnp.int32),
            pltpu.SemaphoreType.DMA((6,)),
            pltpu.SemaphoreType.DMA((1,)),
            pltpu.SemaphoreType.DMA((7,)),
            pltpu.SemaphoreType.DMA((CHUNKS, 3)),
            pltpu.SemaphoreType.DMA((CHUNKS, 8)),
            pltpu.SemaphoreType.DMA((2,)),
            pltpu.SemaphoreType.DMA((7,)),
        ],
        compiler_params=pltpu.CompilerParams(
            collective_id=0, has_side_effects=True, vmem_limit_bytes=51 * 2**20
        ),
        name="layer",
    )(gate_slots, gate_count, down_slots, down_count, inputs, grad_out, gate_blocks, up_blocks, down_blocks)


def save_kernel(
    layer, gate, up, down, out_ref, gradx_ref, gate_out, up_out, down_out, sem
):
    pairs = ((gate, gate_out), (up, up_out), (down, down_out))
    saves = [
        pltpu.make_async_copy(here.at[pl.ds(0, NB)], out, sem.at[n])
        for n, (here, out) in enumerate(pairs)
    ]
    for save in saves:
        save.start()
    out_ref[...] = layer[0]
    gradx_ref[...] = layer[1]
    for save in saves:
        save.wait()


def run_save(layer, *grads):
    vmem = pl.BlockSpec(memory_space=pltpu.VMEM)
    anywhere = pl.BlockSpec(memory_space=pl.ANY)
    tokens = jax.ShapeDtypeStruct((32, WIDTH), BF16)
    blocks = jax.ShapeDtypeStruct((NB, BLOCK, BLOCK), BF16)
    return pl.pallas_call(
        save_kernel,
        out_shape=(tokens, tokens, blocks, blocks, blocks),
        in_specs=[vmem] + [anywhere] * 3,
        out_specs=(vmem, vmem, anywhere, anywhere, anywhere),
        scratch_shapes=[pltpu.SemaphoreType.DMA((3,))],
        compiler_params=pltpu.CompilerParams(vmem_limit_bytes=16 * 2**20),
        name="save",
    )(layer, *grads)


def local(
    inputs,
    grad_out,
    gate_blocks,
    up_blocks,
    down_blocks,
    gate_slots,
    gate_count,
    down_slots,
    down_count,
):
    layer, *grads = run_layer(
        gate_slots,
        gate_count,
        down_slots,
        down_count,
        inputs,
        grad_out,
        gate_blocks[0, 0],
        up_blocks[0, 0],
        down_blocks[0, 0],
    )
    layer_out, grad_x, *grads = run_save(layer, *grads)
    return (layer_out, grad_x) + tuple(grad[None, None] for grad in grads)


def solution(mesh):
    tokens = P("col", "row")
    blocks = P("row", "col", None, None, None)
    slots = P("row", "col", None)
    count = P("row", "col")
    return jax.shard_map(
        local,
        mesh=mesh,
        in_specs=(tokens, tokens, blocks, blocks, blocks, slots, count, slots, count),
        out_specs=(tokens, tokens, blocks, blocks, blocks),
        check_vma=False,
    )
```

```python
import jax
import jax.numpy as jnp
from jax import lax
from jax.experimental import pallas as pl
from jax.experimental.pallas import tpu as pltpu
from jax.sharding import PartitionSpec as P

TOKENS = 256
BLOCK = 128
NB = 96
DPB = 8
FPB = 26
WIDTH = DPB * BLOCK
CHUNK = 2 * BLOCK
CHUNKS = FPB // 2
GROUP = 16
FAR_BIG, FAR_SMALL = 13, 13
LAGS = (0, 4, 8, 12, 16, 20, 24, 28, 32)
MESH = pl.DeviceIdType.MESH
TAIL_SEND = (0,) * 4 + (1,) * 8
TAIL_RECV = tuple(range(8)) + (8,) * 4
HEAD_SEM = (0, 1, 2, 3, 4, 5, 8, 8, 6, 7, 6, 7) + (8,) * 6
SEND_SEM = (0,) * 6 + (1,) * 8 + (2,) * 6
RECV_SEM = (0, 0, 1, 1, 1, 1, 2, 2, 3, 3, 4, 4, 5, 5, 6, 6, 7, 7, 7, 7)
F32 = jnp.float32
BF16 = jnp.bfloat16


def nt_dot(a, b):
    return lax.dot_general(a, b, (((1,), (1,)), ((), ())), preferred_element_type=F32)


def layer_kernel(
    gate_slots,
    gate_count,
    down_slots,
    down_count,
    x_in,
    cot_in,
    gate_in,
    up_in,
    down_in,
    layer_ref,
    raw_gate,
    raw_up,
    raw_down,
    xs,
    w_gate,
    w_up,
    w_down,
    terms,
    half_a,
    full_a,
    sums,
    half_b,
    full_b,
    acts,
    hidden_t,
    pairs,
    x_t,
    cots,
    out_acc,
    gradx_acc,
    tail_out,
    tail,
    tail_core,
    tail_h,
    tail_f,
    tables,
    slot_at,
    load_sem,
    head_send,
    head_recv,
    send_sem,
    recv_sem,
    tail_send,
    tail_recv,
):
    row, col = lax.axis_index("row"), lax.axis_index("col")
    z, y = row // 4, row % 4
    ix, core = col // 2, col % 2

    def y_dev(step):
        return (z * 4 + (y + step) % 4, col)

    def z_dev(step):
        return (((z + step) % 4) * 4 + y, col)

    def x_dev(step):
        return (row, ((ix + step) % 4) * 2 + core)

    sibling = (row, ix * 2 + 1 - core)

    loads = [
        pltpu.make_async_copy(x_in, xs.at[col, 0], load_sem.at[0]),
        pltpu.make_async_copy(cot_in, xs.at[col, 1], load_sem.at[1]),
        pltpu.make_async_copy(gate_in, raw_gate.at[pl.ds(0, NB)], load_sem.at[2]),
        pltpu.make_async_copy(up_in, raw_up.at[pl.ds(0, NB)], load_sem.at[3]),
        pltpu.make_async_copy(down_in, raw_down.at[pl.ds(0, NB)], load_sem.at[4]),
    ]
    loads[0].start()
    loads[1].start()

    barrier = pltpu.get_barrier_semaphore()
    for dev in (y_dev(1), y_dev(3), z_dev(1), z_dev(3), x_dev(1), x_dev(3), sibling):
        pl.semaphore_signal(barrier, inc=1, device_id=dev, device_id_type=MESH)

    zero = jnp.zeros((BLOCK, BLOCK), BF16)
    raw_gate[NB] = zero
    raw_up[NB] = zero
    raw_down[NB] = zero
    out_acc[...] = jnp.zeros_like(out_acc)
    gradx_acc[...] = jnp.zeros_like(gradx_acc)

    pl.semaphore_wait(barrier, 7)

    def head(n, src, dst, dev):
        return pltpu.make_async_remote_copy(
            src_ref=src,
            dst_ref=dst,
            send_sem=head_send.at[0],
            recv_sem=head_recv.at[HEAD_SEM[n]],
            device_id=dev,
            device_id_type=MESH,
        )

    other = 1 - core
    right, left = x_dev(1), x_dev(3)

    def at_x(step, side, arr, rows=pl.ds(0, 32)):
        return xs.at[((ix + step) % 4) * 2 + side, arr, rows]

    def head_start(n, src, dst, dev):
        head(n, src, dst, dev).start()

    def forward(n, ref, dev):
        head_start(n, ref, ref, dev)

    def head_wait(n, ref):
        head(n, ref, ref, right).wait_recv()

    first, second = pl.ds(0, 16), pl.ds(16, 16)
    head_start(0, x_in.at[first], xs.at[col, 0, first], right)
    head_start(1, cot_in.at[first], xs.at[col, 1, first], left)
    head_start(2, x_in.at[second], xs.at[col, 0, second], right)
    head_start(3, cot_in.at[second], xs.at[col, 1, second], left)
    head_start(4, cot_in, xs.at[col, 1], right)
    head_start(5, x_in, xs.at[col, 0], left)
    head_start(6, x_in, xs.at[col, 0], sibling)
    head_start(7, cot_in, xs.at[col, 1], sibling)
    for load in loads[2:]:
        load.start()

    spots = lax.broadcasted_iota(jnp.int32, (8, 128), 0) * 128 + lax.broadcasted_iota(
        jnp.int32, (8, 128), 1
    )

    def enter(n, both):
        gate_tab, down_tab = both
        gate_tab = jnp.where(spots == gate_slots[0, 0, n], n, gate_tab)
        down_tab = jnp.where(spots == down_slots[0, 0, n], n, down_tab)
        return gate_tab, down_tab

    nowhere = jnp.full((8, 128), NB, jnp.int32)
    gate_tab, down_tab = lax.fori_loop(0, NB, enter, (nowhere, nowhere), unroll=8)
    tables[0] = jnp.where(gate_tab < gate_count[0, 0], gate_tab, NB)
    tables[1] = jnp.where(down_tab < down_count[0, 0], down_tab, NB)
    to_scalars = pltpu.make_async_copy(tables, slot_at, load_sem.at[5])
    to_scalars.start()

    def find(table, spot):
        return slot_at[table, spot // 128, spot % 128]

    def place_gate(k, carry):
        for raw, dense in ((raw_gate, w_gate), (raw_up, w_up)):
            for r in range(DPB):
                for b in range(2):
                    slot = find(0, r * FPB + 2 * k + b)
                    dense[k, r * BLOCK : (r + 1) * BLOCK, b * BLOCK : (b + 1) * BLOCK] = raw[slot]
        return carry

    def place_down(k, carry):
        for r in range(DPB):
            for b in range(2):
                slot = find(1, r * FPB + 2 * k + b)
                w_down[k, b * BLOCK : (b + 1) * BLOCK, r * BLOCK : (r + 1) * BLOCK] = raw_down[slot]
        return carry

    to_scalars.wait()
    loads[2].wait()
    loads[3].wait()
    lax.fori_loop(0, 4, place_gate, 0)

    head_wait(0, at_x(3, core, 0, first))
    forward(8, at_x(3, core, 0, first), right)
    head_wait(1, at_x(1, core, 1, first))
    forward(9, at_x(1, core, 1, first), left)
    head_wait(2, at_x(3, core, 0, second))
    forward(10, at_x(3, core, 0, second), right)
    forward(12, at_x(3, core, 0), sibling)
    head_wait(3, at_x(1, core, 1, second))
    forward(11, at_x(1, core, 1, second), left)
    forward(13, at_x(1, core, 1), sibling)

    lax.fori_loop(4, 8, place_gate, 0)

    head_wait(4, at_x(3, core, 1))
    forward(14, at_x(3, core, 1), sibling)
    head_wait(5, at_x(1, core, 0))
    forward(15, at_x(1, core, 0), sibling)

    lax.fori_loop(8, CHUNKS, place_gate, 0)
    loads[4].wait()
    lax.fori_loop(0, 4, place_down, 0)

    head_wait(8, at_x(2, core, 0))
    forward(16, at_x(2, core, 0), sibling)
    head_wait(9, at_x(2, core, 1))
    forward(17, at_x(2, core, 1), sibling)

    lax.fori_loop(4, CHUNKS, place_down, 0)

    head_wait(6, xs.at[pl.ds(0, 4)])
    loads[0].wait()
    loads[1].wait()

    def lay_out_inputs():
        for r in range(DPB):
            cols = slice(r * BLOCK, (r + 1) * BLOCK)
            x_t[r] = xs[:, 0, :, cols].reshape(TOKENS, BLOCK).T
            cots[r] = xs[:, 1, :, cols].reshape(TOKENS, BLOCK)

    def places(k):
        odd = k % 2
        i = (1 - odd) * y + odd * z
        j = (1 - odd) * z + odd * y

        def dev(step, along_z):
            y_new = (y + (1 - along_z) * step) % 4
            z_new = (z + along_z * step) % 4
            return (z_new * 4 + y_new, col)

        return i, j, dev(1, odd), dev(3, odd), dev(1, 1 - odd), dev(3, 1 - odd)

    def far(k, along_a):
        along_z = swap(k, k % 2, 1 - k % 2)[1 - along_a]
        return ((z + 2 * along_z) % 4 * 4 + (y + 2 * (1 - along_z)) % 4, col)

    def swap(k, a, b):
        turned = k // (CHUNKS - 1)
        return (1 - turned) * a + turned * b, (1 - turned) * b + turned * a

    def gather_places(k):
        i, j, ar, al, br, bl = places(k)
        p, q = swap(k, i, j)
        pick = lambda a, b: tuple(swap(k, m, n)[0] for m, n in zip(a, b))
        return p, q, pick(ar, br), pick(al, bl), pick(br, ar), pick(bl, al)

    def choose(late, a, b):
        if isinstance(a, tuple):
            return tuple(choose(late, m, n) for m, n in zip(a, b))
        return late * a + (1 - late) * b

    def copy(k, n, src, dst, dev):
        return pltpu.make_async_remote_copy(
            src_ref=src,
            dst_ref=dst,
            send_sem=send_sem.at[SEND_SEM[n]],
            recv_sem=recv_sem.at[k, RECV_SEM[n]],
            device_id=dev,
            device_id_type=MESH,
        )

    def all_copies(k):
        i, j, ar, al, br, bl = places(k)
        i1, i2, i3 = (i + 1) % 4, (i + 2) % 4, (i + 3) % 4
        j1, j2, j3 = (j + 1) % 4, (j + 2) % 4, (j + 3) % 4
        p, q, p_right, p_left, q_right, q_left = gather_places(k)
        p1, p3, q1, q3 = (p + 1) % 4, (p + 3) % 4, (q + 1) % 4, (q + 3) % 4
        same = lambda n, ref, dev: copy(k, n, ref, ref, dev)
        near, rest = pl.ds(0, 2), pl.ds(2, 2)
        big = (k + CHUNKS - FAR_BIG) // CHUNKS
        small = (k + CHUNKS - FAR_SMALL) // CHUNKS
        far_big, far_small = far(k, 1), far(k, 0)
        return [
            lambda: copy(k, 0, terms.at[k, i2, 0], half_a.at[k, 0], ar),
            lambda: copy(k, 1, terms.at[k, i2, 1], half_a.at[k, 1], al),
            lambda: copy(k, 2, terms.at[k, i1, 1], full_a.at[k, 0, 1], ar),
            lambda: copy(k, 3, terms.at[k, i3, 0], full_a.at[k, 1, 0], al),
            lambda: copy(k, 4, terms.at[k, i1, 0], full_a.at[k, 0, 0], ar),
            lambda: copy(k, 5, terms.at[k, i3, 1], full_a.at[k, 1, 1], al),
            lambda: copy(k, 6, sums.at[k, j2, 0], half_b.at[k, 0], br),
            lambda: copy(k, 7, sums.at[k, j2, 1], half_b.at[k, 1], bl),
            lambda: copy(k, 8, sums.at[k, j1], full_b.at[k, 0], br),
            lambda: copy(k, 9, sums.at[k, j3], full_b.at[k, 1], bl),
            lambda: same(10, acts.at[k, p, q], q_right),
            lambda: same(11, acts.at[k, p, q], q_left),
            lambda: same(12, acts.at[k, p, choose(small, q, q3), 0], choose(small, far_small, q_right)),
            lambda: same(13, acts.at[k, p, choose(small, q, q1), 1], choose(small, far_small, q_left)),
            lambda: same(14, acts.at[k, p, near], p_right),
            lambda: same(15, acts.at[k, p, rest], p_left),
            lambda: same(16, acts.at[k, p, rest], p_right),
            lambda: same(17, acts.at[k, p, near], p_left),
            lambda: same(18, acts.at[k, choose(big, p, p3), near], choose(big, far_big, p_right)),
            lambda: same(19, acts.at[k, choose(big, p, p1), rest], choose(big, far_big, p_left)),
        ]

    def arrived(k, n, ref):
        i, j, ar, al, br, bl = places(k)
        copy(k, n, ref, ref, ar).wait_recv()

    def plus(a, b):
        return (a.astype(F32) + b.astype(F32)).astype(BF16)

    def p0(k):
        for part, (arr, weights) in enumerate(((0, w_gate), (0, w_up), (1, w_down))):
            if part < 2:
                lhs = xs[:, 0].reshape(TOKENS, WIDTH)
                val = jnp.dot(lhs, weights[k], preferred_element_type=F32)
            else:
                lhs = xs[:, 1].reshape(TOKENS, WIDTH)
                val = nt_dot(lhs, weights[k])
            val = val.astype(BF16)
            for b in range(2):
                terms[k, :, b, :, part * 16 : (part + 1) * 16, :] = val[
                    :, b * BLOCK : (b + 1) * BLOCK
                ].reshape(4, 4, 16, BLOCK)
        copies = all_copies(k)
        for n in range(4):
            copies[n]().start()

    def p1(k):
        i, j, *_ = places(k)
        i1, i3 = (i + 1) % 4, (i + 3) % 4
        copies = all_copies(k)
        arrived(k, 0, half_a.at[k])
        terms[k, i1, 0] = plus(terms[k, i1, 0], half_a[k, 0])
        copies[4]().start()
        terms[k, i3, 1] = plus(terms[k, i3, 1], half_a[k, 1])
        copies[5]().start()

    def p2(k):
        i, j, *_ = places(k)
        copies = all_copies(k)
        arrived(k, 2, full_a.at[k])
        for b in range(2):
            total = terms[k, i, b].astype(F32) + full_a[k, 0, b].astype(F32)
            sums[k, :, b] = (total + full_a[k, 1, b].astype(F32)).astype(BF16)
        copies[6]().start()
        copies[7]().start()

    def p3(k):
        i, j, *_ = places(k)
        j1, j3 = (j + 1) % 4, (j + 3) % 4
        copies = all_copies(k)
        arrived(k, 6, half_b.at[k])
        sums[k, j1, 0] = plus(sums[k, j1, 0], half_b[k, 0])
        copies[8]().start()
        sums[k, j3, 1] = plus(sums[k, j3, 1], half_b[k, 1])
        copies[9]().start()

    def p4(k):
        i, j, *_ = places(k)
        p, q, *_ = gather_places(k)
        copies = all_copies(k)
        arrived(k, 8, full_b.at[k])
        total = sums[k, j].astype(F32) + full_b[k, 0].astype(F32) + full_b[k, 1].astype(F32)
        gate, up, grad = total[:, 0:16], total[:, 16:32], total[:, 32:48]
        sigma = 1.0 / (1.0 + jnp.exp(-gate))
        acts[k, p, q, :, 0:16, :] = (gate * sigma * up).astype(BF16)
        acts[k, p, q, :, 16:32, :] = (grad * up * sigma * (1.0 + gate * (1.0 - sigma))).astype(BF16)
        acts[k, p, q, :, 32:48, :] = (grad * gate * sigma).astype(BF16)
        copies[10]().start()
        copies[11]().start()

        @pl.when(k >= FAR_SMALL)
        def _():
            copies[12]().start()
            copies[13]().start()

    def p5(k):
        p, q, *_ = gather_places(k)
        copies = all_copies(k)
        arrived(k, 10, acts.at[k, p, pl.ds(0, 2)])

        @pl.when(k < FAR_SMALL)
        def _():
            copies[12]().start()
            copies[13]().start()

    def p6(k):
        p, q, *_ = gather_places(k)
        copies = all_copies(k)
        arrived(k, 12, acts.at[k, p, 0])
        for n in range(14, 18):
            copies[n]().start()

        @pl.when(k >= FAR_BIG)
        def _():
            copies[18]().start()
            copies[19]().start()

    def p7(k):
        p, q, *_ = gather_places(k)
        copies = all_copies(k)
        arrived(k, 14, acts.at[k, 0])

        @pl.when(k < FAR_BIG)
        def _():
            copies[18]().start()
            copies[19]().start()

    def p8(k):
        p, q, *_ = gather_places(k)
        arrived(k, 16, acts.at[k, pl.ds(0, 2)])

        groups = [swap(k, a, b) for a in range(4) for b in range(4)]

        def act(part):
            cols = [
                jnp.concatenate([acts[k, u, v, b, part * 16 : (part + 1) * 16, :] for u, v in groups])
                for b in range(2)
            ]
            return cols, jnp.concatenate(cols, axis=1)

        (_, hidden), (gate_cols, grad_gate), (up_cols, grad_up) = act(0), act(1), act(2)
        for n in range(4):
            cols = slice(n * 256, (n + 1) * 256)
            out = jnp.dot(hidden, w_down[k, :, cols], preferred_element_type=F32)
            out_acc[:, :, cols] += out.reshape(8, 32, 256)
            grad = nt_dot(grad_gate, w_gate[k, cols, :]) + nt_dot(grad_up, w_up[k, cols, :])
            gradx_acc[:, :, cols] += grad.reshape(8, 32, 256)
        hidden_t[pl.ds(2 * k, 2)] = hidden.T.reshape(2, BLOCK, TOKENS)
        for b in range(2):
            pairs[2 * k + b, :, 0:BLOCK] = gate_cols[b]
            pairs[2 * k + b, :, BLOCK:] = up_cols[b]

    def tick(t, carry):
        for phase, late in zip((p7, p6, p5, p4, p3, p2, p1, p0, p8), LAGS[7::-1] + LAGS[8:]):
            k = t - late

            @pl.when(jnp.logical_and(k >= 0, k < CHUNKS))
            def _():
                phase(k)

        @pl.when(t == 6)
        def _():
            lay_out_inputs()

        return carry

    lax.fori_loop(0, CHUNKS + LAGS[8], tick, 0)

    def down_group(g, carry):
        for u in range(GROUP):
            n = g * GROUP + u
            spot = down_slots[0, 0, n]
            val = jnp.dot(hidden_t[spot % FPB], cots[spot // FPB], preferred_element_type=F32)
            raw_down[n] = jnp.where(n < down_count[0, 0], val, 0.0).astype(BF16)
        return carry

    def gate_group(g, carry):
        for u in range(GROUP):
            n = g * GROUP + u
            spot = gate_slots[0, 0, n]
            val = jnp.dot(x_t[spot // FPB], pairs[spot % FPB], preferred_element_type=F32)
            val = jnp.where(n < gate_count[0, 0], val, 0.0).astype(BF16)
            raw_gate[n] = val[:, 0:BLOCK]
            raw_up[n] = val[:, BLOCK:]
        return carry

    def last(n, src, dst, dev):
        return pltpu.make_async_remote_copy(
            src_ref=src,
            dst_ref=dst,
            send_sem=tail_send.at[TAIL_SEND[n]],
            recv_sem=tail_recv.at[TAIL_RECV[n]],
            device_id=dev,
            device_id_type=MESH,
        )

    x0, x1, x2, x3 = ix, (ix + 1) % 4, (ix + 2) % 4, (ix + 3) % 4
    totals = (out_acc, gradx_acc)
    cores = {}
    for n, at in ((0, x2), (1, x1), (2, x3), (3, x0)):
        for arr in range(2):
            tail_out[at, arr] = totals[arr][at * 2 + other].astype(BF16)
        cores[n] = last(n, tail_out.at[at], tail_core.at[at], sibling)
        cores[n].start()

    def both(n, at):
        cores[n].wait_recv()
        for arr in range(2):
            mine = totals[arr][at * 2 + core] + tail_core[at, arr].astype(F32)
            tail[at, arr] = mine.astype(BF16)

    halves = (pl.ds(0, 16), pl.ds(16, 16))
    steps = (
        [last(4 + h, tail.at[x2, 0, rows], tail_h.at[0, rows], right) for h, rows in enumerate(halves)]
        + [last(6 + h, tail.at[x2, 1, rows], tail_h.at[1, rows], left) for h, rows in enumerate(halves)]
        + [
            last(8, tail.at[x1, 1], tail_f.at[0, 1], right),
            last(9, tail.at[x3, 0], tail_f.at[1, 0], left),
        ]
        + [last(10, tail.at[x1, 0, rows], tail_f.at[0, 0, rows], right) for rows in halves]
        + [last(11, tail.at[x3, 1, rows], tail_f.at[1, 1, rows], left) for rows in halves]
    )
    lax.fori_loop(0, 2, down_group, 0)
    both(0, x2)
    for n in range(4):
        steps[n].start()
    both(1, x1)
    steps[4].start()
    both(2, x3)
    steps[5].start()
    lax.fori_loop(2, 6, down_group, 0)
    lax.fori_loop(0, 2, gate_group, 0)
    for h, rows in enumerate(halves):
        steps[h].wait_recv()
        tail[x1, 0, rows] = plus(tail[x1, 0, rows], tail_h[0, rows])
        steps[6 + h].start()
        steps[2 + h].wait_recv()
        tail[x3, 1, rows] = plus(tail[x3, 1, rows], tail_h[1, rows])
        steps[8 + h].start()
    lax.fori_loop(2, 6, gate_group, 0)
    cores[3].wait_recv()
    last(8, tail_f, tail_f, right).wait_recv()
    for arr in range(2):
        total = totals[arr][x0 * 2 + core] + tail_core[x0, arr].astype(F32)
        total = total + tail_f[0, arr].astype(F32) + tail_f[1, arr].astype(F32)
        layer_ref[arr] = total.astype(BF16)

    most = terms.at[:, pl.ds(0, 3)]
    copy(0, 0, most, most, right).wait_send()
    copy(0, 6, terms.at[:, pl.ds(0, 3), 0], terms.at[:, pl.ds(0, 3), 0], right).wait_send()
    copy(0, 14, most, most, right).wait_send()
    last(0, tail_out, tail_core, sibling).wait_send()
    last(4, tail.at[pl.ds(0, 3)], tail.at[pl.ds(0, 3)], right).wait_send()
    head(0, xs.at[pl.ds(0, 7)], xs.at[pl.ds(0, 7)], right).wait_send()


def run_layer(gate_slots, gate_count, down_slots, down_count, inputs, grad_out, gate_blocks, up_blocks, down_blocks):
    anywhere = pl.BlockSpec(memory_space=pl.ANY)
    scalars = pl.BlockSpec(memory_space=pltpu.SMEM)
    vmem = pl.BlockSpec(memory_space=pltpu.VMEM)
    raw = pltpu.VMEM((NB + 1, BLOCK, BLOCK), BF16)
    part = (48, BLOCK)
    return pl.pallas_call(
        layer_kernel,
        out_shape=(
            pltpu.VMEM((2, 32, WIDTH), BF16),
            raw,
            raw,
            raw,
        ),
        in_specs=[scalars] * 4 + [anywhere] * 5,
        out_specs=(vmem,) * 4,
        scratch_shapes=[
            pltpu.VMEM((8, 2, 32, WIDTH), BF16),
            pltpu.VMEM((CHUNKS, WIDTH, CHUNK), BF16),
            pltpu.VMEM((CHUNKS, WIDTH, CHUNK), BF16),
            pltpu.VMEM((CHUNKS, CHUNK, WIDTH), BF16),
            pltpu.VMEM((CHUNKS, 4, 2, 4) + part, BF16),
            pltpu.VMEM((CHUNKS, 2, 4) + part, BF16),
            pltpu.VMEM((CHUNKS, 2, 2, 4) + part, BF16),
            pltpu.VMEM((CHUNKS, 4, 2) + part, BF16),
            pltpu.VMEM((CHUNKS, 2) + part, BF16),
            pltpu.VMEM((CHUNKS, 2, 2) + part, BF16),
            pltpu.VMEM((CHUNKS, 4, 4, 2) + part, BF16),
            pltpu.VMEM((FPB, BLOCK, TOKENS), BF16),
            pltpu.VMEM((FPB, TOKENS, 2 * BLOCK), BF16),
            pltpu.VMEM((DPB, BLOCK, TOKENS), BF16),
            pltpu.VMEM((DPB, TOKENS, BLOCK), BF16),
            pltpu.VMEM((8, 32, WIDTH), F32),
            pltpu.VMEM((8, 32, WIDTH), F32),
            pltpu.VMEM((4, 2, 32, WIDTH), BF16),
            pltpu.VMEM((4, 2, 32, WIDTH), BF16),
            pltpu.VMEM((4, 2, 32, WIDTH), BF16),
            pltpu.VMEM((2, 32, WIDTH), BF16),
            pltpu.VMEM((2, 2, 32, WIDTH), BF16),
            pltpu.VMEM((2, 8, 128), jnp.int32),
            pltpu.SMEM((2, 8, 128), jnp.int32),
            pltpu.SemaphoreType.DMA((6,)),
            pltpu.SemaphoreType.DMA((1,)),
            pltpu.SemaphoreType.DMA((9,)),
            pltpu.SemaphoreType.DMA((3,)),
            pltpu.SemaphoreType.DMA((CHUNKS, 8)),
            pltpu.SemaphoreType.DMA((2,)),
            pltpu.SemaphoreType.DMA((9,)),
        ],
        compiler_params=pltpu.CompilerParams(
            collective_id=0, has_side_effects=True, vmem_limit_bytes=51 * 2**20
        ),
        name="layer",
    )(gate_slots, gate_count, down_slots, down_count, inputs, grad_out, gate_blocks, up_blocks, down_blocks)


def save_kernel(
    layer, gate, up, down, out_ref, gradx_ref, gate_out, up_out, down_out, sem
):
    pairs = ((gate, gate_out), (up, up_out), (down, down_out))
    quarters = [pl.ds(q * (NB // 4), NB // 4) for q in range(4)]
    saves = [
        pltpu.make_async_copy(here.at[rows], out.at[rows], sem.at[n, q])
        for q, rows in enumerate(quarters)
        for n, (here, out) in enumerate(pairs)
    ]
    for save in saves:
        save.start()
    out_ref[...] = layer[0]
    gradx_ref[...] = layer[1]
    for save in saves:
        save.wait()


def run_save(layer, *grads):
    vmem = pl.BlockSpec(memory_space=pltpu.VMEM)
    anywhere = pl.BlockSpec(memory_space=pl.ANY)
    tokens = jax.ShapeDtypeStruct((32, WIDTH), BF16)
    blocks = jax.ShapeDtypeStruct((NB, BLOCK, BLOCK), BF16)
    return pl.pallas_call(
        save_kernel,
        out_shape=(tokens, tokens, blocks, blocks, blocks),
        in_specs=[vmem] + [anywhere] * 3,
        out_specs=(vmem, vmem, anywhere, anywhere, anywhere),
        scratch_shapes=[pltpu.SemaphoreType.DMA((3, 4))],
        compiler_params=pltpu.CompilerParams(vmem_limit_bytes=16 * 2**20),
        name="save",
    )(layer, *grads)


def local(
    inputs,
    grad_out,
    gate_blocks,
    up_blocks,
    down_blocks,
    gate_slots,
    gate_count,
    down_slots,
    down_count,
):
    layer, *grads = run_layer(
        gate_slots,
        gate_count,
        down_slots,
        down_count,
        inputs,
        grad_out,
        gate_blocks[0, 0],
        up_blocks[0, 0],
        down_blocks[0, 0],
    )
    layer_out, grad_x, *grads = run_save(layer, *grads)
    return (layer_out, grad_x) + tuple(grad[None, None] for grad in grads)


def solution(mesh):
    tokens = P("col", "row")
    blocks = P("row", "col", None, None, None)
    slots = P("row", "col", None)
    count = P("row", "col")
    return jax.shard_map(
        local,
        mesh=mesh,
        in_specs=(tokens, tokens, blocks, blocks, blocks, slots, count, slots, count),
        out_specs=(tokens, tokens, blocks, blocks, blocks),
        check_vma=False,
    )
```

```python
import jax
import jax.numpy as jnp
from jax import lax
from jax.experimental import pallas as pl
from jax.experimental.pallas import tpu as pltpu
from jax.sharding import PartitionSpec as P

TOKENS = 256
BLOCK = 128
NB = 96
DPB = 8
FPB = 26
WIDTH = DPB * BLOCK
CHUNK = 2 * BLOCK
CHUNKS = FPB // 2
GROUP = 16
LAGS = (0, 4, 8, 12, 16, 20, 24, 28, 32)
MESH = pl.DeviceIdType.MESH
TAIL_SEND = (0,) * 4 + (1,) * 8
TAIL_RECV = tuple(range(8)) + (8,) * 4
HEAD_SEM = (0, 1, 2, 3, 4, 5, 8, 8, 6, 7, 6, 7) + (8,) * 6
SEND_SEM = (0,) * 6 + (1,) * 8 + (2,) * 6
RECV_SEM = (0, 0, 1, 1, 1, 1, 2, 2, 3, 3, 4, 4, 5, 5, 6, 6, 7, 7, 7, 7)
F32 = jnp.float32
BF16 = jnp.bfloat16


def nt_dot(a, b):
    return lax.dot_general(a, b, (((1,), (1,)), ((), ())), preferred_element_type=F32)


def layer_kernel(
    gate_slots,
    gate_count,
    down_slots,
    down_count,
    x_in,
    cot_in,
    gate_in,
    up_in,
    down_in,
    layer_ref,
    raw_gate,
    raw_up,
    raw_down,
    xs,
    w_gate,
    w_up,
    w_down,
    terms,
    half_a,
    full_a,
    sums,
    half_b,
    full_b,
    acts,
    hidden_t,
    pairs,
    x_t,
    cots,
    out_acc,
    gradx_acc,
    tail_out,
    tail,
    tail_core,
    tail_h,
    tail_f,
    tables,
    slot_at,
    load_sem,
    head_send,
    head_recv,
    send_sem,
    recv_sem,
    tail_send,
    tail_recv,
):
    row, col = lax.axis_index("row"), lax.axis_index("col")
    z, y = row // 4, row % 4
    ix, core = col // 2, col % 2

    def y_dev(step):
        return (z * 4 + (y + step) % 4, col)

    def z_dev(step):
        return (((z + step) % 4) * 4 + y, col)

    def x_dev(step):
        return (row, ((ix + step) % 4) * 2 + core)

    sibling = (row, ix * 2 + 1 - core)

    loads = [
        pltpu.make_async_copy(x_in, xs.at[col, 0], load_sem.at[0]),
        pltpu.make_async_copy(cot_in, xs.at[col, 1], load_sem.at[1]),
        pltpu.make_async_copy(gate_in, raw_gate.at[pl.ds(0, NB)], load_sem.at[2]),
        pltpu.make_async_copy(up_in, raw_up.at[pl.ds(0, NB)], load_sem.at[3]),
        pltpu.make_async_copy(down_in, raw_down.at[pl.ds(0, NB)], load_sem.at[4]),
    ]
    loads[0].start()
    loads[1].start()

    barrier = pltpu.get_barrier_semaphore()
    for dev in (y_dev(1), y_dev(3), z_dev(1), z_dev(3), x_dev(1), x_dev(3), sibling):
        pl.semaphore_signal(barrier, inc=1, device_id=dev, device_id_type=MESH)

    zero = jnp.zeros((BLOCK, BLOCK), BF16)
    raw_gate[NB] = zero
    raw_up[NB] = zero
    raw_down[NB] = zero
    out_acc[...] = jnp.zeros_like(out_acc)
    gradx_acc[...] = jnp.zeros_like(gradx_acc)

    pl.semaphore_wait(barrier, 7)

    def head(n, src, dst, dev):
        return pltpu.make_async_remote_copy(
            src_ref=src,
            dst_ref=dst,
            send_sem=head_send.at[0],
            recv_sem=head_recv.at[HEAD_SEM[n]],
            device_id=dev,
            device_id_type=MESH,
        )

    other = 1 - core
    right, left = x_dev(1), x_dev(3)

    def at_x(step, side, arr, rows=pl.ds(0, 32)):
        return xs.at[((ix + step) % 4) * 2 + side, arr, rows]

    def head_start(n, src, dst, dev):
        head(n, src, dst, dev).start()

    def forward(n, ref, dev):
        head_start(n, ref, ref, dev)

    def head_wait(n, ref):
        head(n, ref, ref, right).wait_recv()

    first, second = pl.ds(0, 16), pl.ds(16, 16)
    head_start(0, x_in.at[first], xs.at[col, 0, first], right)
    head_start(1, cot_in.at[first], xs.at[col, 1, first], left)
    head_start(2, x_in.at[second], xs.at[col, 0, second], right)
    head_start(3, cot_in.at[second], xs.at[col, 1, second], left)
    head_start(4, cot_in, xs.at[col, 1], right)
    head_start(5, x_in, xs.at[col, 0], left)
    head_start(6, x_in, xs.at[col, 0], sibling)
    head_start(7, cot_in, xs.at[col, 1], sibling)
    for load in loads[2:]:
        load.start()

    spots = lax.broadcasted_iota(jnp.int32, (8, 128), 0) * 128 + lax.broadcasted_iota(
        jnp.int32, (8, 128), 1
    )

    def enter(n, both):
        gate_tab, down_tab = both
        gate_tab = jnp.where(spots == gate_slots[0, 0, n], n, gate_tab)
        down_tab = jnp.where(spots == down_slots[0, 0, n], n, down_tab)
        return gate_tab, down_tab

    nowhere = jnp.full((8, 128), NB, jnp.int32)
    gate_tab, down_tab = lax.fori_loop(0, NB, enter, (nowhere, nowhere), unroll=8)
    tables[0] = jnp.where(gate_tab < gate_count[0, 0], gate_tab, NB)
    tables[1] = jnp.where(down_tab < down_count[0, 0], down_tab, NB)
    to_scalars = pltpu.make_async_copy(tables, slot_at, load_sem.at[5])
    to_scalars.start()

    def find(table, spot):
        return slot_at[table, spot // 128, spot % 128]

    def place_gate(k, carry):
        for raw, dense in ((raw_gate, w_gate), (raw_up, w_up)):
            for r in range(DPB):
                for b in range(2):
                    slot = find(0, r * FPB + 2 * k + b)
                    dense[k, r * BLOCK : (r + 1) * BLOCK, b * BLOCK : (b + 1) * BLOCK] = raw[slot]
        return carry

    def place_down(k, carry):
        for r in range(DPB):
            for b in range(2):
                slot = find(1, r * FPB + 2 * k + b)
                w_down[k, b * BLOCK : (b + 1) * BLOCK, r * BLOCK : (r + 1) * BLOCK] = raw_down[slot]
        return carry

    to_scalars.wait()
    loads[2].wait()
    loads[3].wait()
    lax.fori_loop(0, 4, place_gate, 0)

    head_wait(0, at_x(3, core, 0, first))
    forward(8, at_x(3, core, 0, first), right)
    head_wait(1, at_x(1, core, 1, first))
    forward(9, at_x(1, core, 1, first), left)
    head_wait(2, at_x(3, core, 0, second))
    forward(10, at_x(3, core, 0, second), right)
    forward(12, at_x(3, core, 0), sibling)
    head_wait(3, at_x(1, core, 1, second))
    forward(11, at_x(1, core, 1, second), left)
    forward(13, at_x(1, core, 1), sibling)

    lax.fori_loop(4, 8, place_gate, 0)

    head_wait(4, at_x(3, core, 1))
    forward(14, at_x(3, core, 1), sibling)
    head_wait(5, at_x(1, core, 0))
    forward(15, at_x(1, core, 0), sibling)

    lax.fori_loop(8, CHUNKS, place_gate, 0)
    loads[4].wait()
    lax.fori_loop(0, 4, place_down, 0)

    head_wait(8, at_x(2, core, 0))
    forward(16, at_x(2, core, 0), sibling)
    head_wait(9, at_x(2, core, 1))
    forward(17, at_x(2, core, 1), sibling)

    lax.fori_loop(4, CHUNKS, place_down, 0)

    head_wait(6, xs.at[pl.ds(0, 4)])
    loads[0].wait()
    loads[1].wait()

    def lay_out_inputs():
        for r in range(DPB):
            cols = slice(r * BLOCK, (r + 1) * BLOCK)
            x_t[r] = xs[:, 0, :, cols].reshape(TOKENS, BLOCK).T
            cots[r] = xs[:, 1, :, cols].reshape(TOKENS, BLOCK)

    def places(k):
        odd = (k + core) % 2
        i = (1 - odd) * y + odd * z
        j = (1 - odd) * z + odd * y

        def dev(step, along_z):
            y_new = (y + (1 - along_z) * step) % 4
            z_new = (z + along_z * step) % 4
            return (z_new * 4 + y_new, col)

        return i, j, dev(1, odd), dev(3, odd), dev(1, 1 - odd), dev(3, 1 - odd)

    def copy(k, n, src, dst, dev):
        return pltpu.make_async_remote_copy(
            src_ref=src,
            dst_ref=dst,
            send_sem=send_sem.at[SEND_SEM[n]],
            recv_sem=recv_sem.at[k, RECV_SEM[n]],
            device_id=dev,
            device_id_type=MESH,
        )

    def all_copies(k):
        i, j, ar, al, br, bl = places(k)
        i1, i2, i3 = (i + 1) % 4, (i + 2) % 4, (i + 3) % 4
        j1, j2, j3 = (j + 1) % 4, (j + 2) % 4, (j + 3) % 4
        same = lambda n, ref, dev: copy(k, n, ref, ref, dev)
        near, rest = pl.ds(0, 2), pl.ds(2, 2)
        return [
            lambda: copy(k, 0, terms.at[k, i2, 0], half_a.at[k, 0], ar),
            lambda: copy(k, 1, terms.at[k, i2, 1], half_a.at[k, 1], al),
            lambda: copy(k, 2, terms.at[k, i1, 1], full_a.at[k, 0, 1], ar),
            lambda: copy(k, 3, terms.at[k, i3, 0], full_a.at[k, 1, 0], al),
            lambda: copy(k, 4, terms.at[k, i1, 0], full_a.at[k, 0, 0], ar),
            lambda: copy(k, 5, terms.at[k, i3, 1], full_a.at[k, 1, 1], al),
            lambda: copy(k, 6, sums.at[k, j2, 0], half_b.at[k, 0], br),
            lambda: copy(k, 7, sums.at[k, j2, 1], half_b.at[k, 1], bl),
            lambda: copy(k, 8, sums.at[k, j1], full_b.at[k, 0], br),
            lambda: copy(k, 9, sums.at[k, j3], full_b.at[k, 1], bl),
            lambda: same(10, acts.at[k, i, j], br),
            lambda: same(11, acts.at[k, i, j], bl),
            lambda: same(12, acts.at[k, i, j3, 0], br),
            lambda: same(13, acts.at[k, i, j1, 1], bl),
            lambda: same(14, acts.at[k, i, near], ar),
            lambda: same(15, acts.at[k, i, rest], al),
            lambda: same(16, acts.at[k, i, rest], ar),
            lambda: same(17, acts.at[k, i, near], al),
            lambda: same(18, acts.at[k, i3, near], ar),
            lambda: same(19, acts.at[k, i1, rest], al),
        ]

    def arrived(k, n, ref):
        i, j, ar, al, br, bl = places(k)
        copy(k, n, ref, ref, ar).wait_recv()

    def plus(a, b):
        return (a.astype(F32) + b.astype(F32)).astype(BF16)

    def p0(k):
        for part, (arr, weights) in enumerate(((0, w_gate), (0, w_up), (1, w_down))):
            if part < 2:
                lhs = xs[:, 0].reshape(TOKENS, WIDTH)
                val = jnp.dot(lhs, weights[k], preferred_element_type=F32)
            else:
                lhs = xs[:, 1].reshape(TOKENS, WIDTH)
                val = nt_dot(lhs, weights[k])
            val = val.astype(BF16)
            for b in range(2):
                terms[k, :, b, :, part * 16 : (part + 1) * 16, :] = val[
                    :, b * BLOCK : (b + 1) * BLOCK
                ].reshape(4, 4, 16, BLOCK)
        copies = all_copies(k)
        for n in range(4):
            copies[n]().start()

    def p1(k):
        i, j, *_ = places(k)
        i1, i3 = (i + 1) % 4, (i + 3) % 4
        copies = all_copies(k)
        arrived(k, 0, half_a.at[k])
        terms[k, i1, 0] = plus(terms[k, i1, 0], half_a[k, 0])
        copies[4]().start()
        terms[k, i3, 1] = plus(terms[k, i3, 1], half_a[k, 1])
        copies[5]().start()

    def p2(k):
        i, j, *_ = places(k)
        copies = all_copies(k)
        arrived(k, 2, full_a.at[k])
        for b in range(2):
            total = terms[k, i, b].astype(F32) + full_a[k, 0, b].astype(F32)
            sums[k, :, b] = (total + full_a[k, 1, b].astype(F32)).astype(BF16)
        copies[6]().start()
        copies[7]().start()

    def p3(k):
        i, j, *_ = places(k)
        j1, j3 = (j + 1) % 4, (j + 3) % 4
        copies = all_copies(k)
        arrived(k, 6, half_b.at[k])
        sums[k, j1, 0] = plus(sums[k, j1, 0], half_b[k, 0])
        copies[8]().start()
        sums[k, j3, 1] = plus(sums[k, j3, 1], half_b[k, 1])
        copies[9]().start()

    def p4(k):
        i, j, *_ = places(k)
        copies = all_copies(k)
        arrived(k, 8, full_b.at[k])
        total = sums[k, j].astype(F32) + full_b[k, 0].astype(F32) + full_b[k, 1].astype(F32)
        gate, up, grad = total[:, 0:16], total[:, 16:32], total[:, 32:48]
        sigma = 1.0 / (1.0 + jnp.exp(-gate))
        acts[k, i, j, :, 0:16, :] = (gate * sigma * up).astype(BF16)
        acts[k, i, j, :, 16:32, :] = (grad * up * sigma * (1.0 + gate * (1.0 - sigma))).astype(BF16)
        acts[k, i, j, :, 32:48, :] = (grad * gate * sigma).astype(BF16)
        copies[10]().start()
        copies[11]().start()

    def p5(k):
        i, j, *_ = places(k)
        copies = all_copies(k)
        arrived(k, 10, acts.at[k, i, pl.ds(0, 2)])
        copies[12]().start()
        copies[13]().start()

    def p6(k):
        i, j, *_ = places(k)
        copies = all_copies(k)
        arrived(k, 12, acts.at[k, i, 0])
        for n in range(14, 18):
            copies[n]().start()

    def p7(k):
        i, j, *_ = places(k)
        copies = all_copies(k)
        arrived(k, 14, acts.at[k, 0])
        copies[18]().start()
        copies[19]().start()

    def p8(k):
        i, j, *_ = places(k)
        arrived(k, 16, acts.at[k, pl.ds(0, 2)])

        def act(part):
            cols = [
                acts[k, :, :, b, part * 16 : (part + 1) * 16, :].reshape(TOKENS, BLOCK)
                for b in range(2)
            ]
            return cols, jnp.concatenate(cols, axis=1)

        (_, hidden), (gate_cols, grad_gate), (up_cols, grad_up) = act(0), act(1), act(2)
        for n in range(4):
            cols = slice(n * 256, (n + 1) * 256)
            out = jnp.dot(hidden, w_down[k, :, cols], preferred_element_type=F32)
            out_acc[:, :, cols] += out.reshape(8, 32, 256)
            grad = nt_dot(grad_gate, w_gate[k, cols, :]) + nt_dot(grad_up, w_up[k, cols, :])
            gradx_acc[:, :, cols] += grad.reshape(8, 32, 256)
        hidden_t[pl.ds(2 * k, 2)] = hidden.T.reshape(2, BLOCK, TOKENS)
        for b in range(2):
            pairs[2 * k + b, :, 0:BLOCK] = gate_cols[b]
            pairs[2 * k + b, :, BLOCK:] = up_cols[b]

    def tick(t, carry):
        for phase, late in zip((p7, p6, p5, p4, p3, p2, p1, p0, p8), LAGS[7::-1] + LAGS[8:]):
            k = t - late

            @pl.when(jnp.logical_and(k >= 0, k < CHUNKS))
            def _():
                phase(k)

        @pl.when(t == 6)
        def _():
            lay_out_inputs()

        return carry

    lax.fori_loop(0, CHUNKS + LAGS[8], tick, 0)

    def down_group(g, carry):
        for u in range(GROUP):
            n = g * GROUP + u
            spot = down_slots[0, 0, n]
            val = jnp.dot(hidden_t[spot % FPB], cots[spot // FPB], preferred_element_type=F32)
            raw_down[n] = jnp.where(n < down_count[0, 0], val, 0.0).astype(BF16)
        return carry

    def gate_group(g, carry):
        for u in range(GROUP):
            n = g * GROUP + u
            spot = gate_slots[0, 0, n]
            val = jnp.dot(x_t[spot // FPB], pairs[spot % FPB], preferred_element_type=F32)
            val = jnp.where(n < gate_count[0, 0], val, 0.0).astype(BF16)
            raw_gate[n] = val[:, 0:BLOCK]
            raw_up[n] = val[:, BLOCK:]
        return carry

    def last(n, src, dst, dev):
        return pltpu.make_async_remote_copy(
            src_ref=src,
            dst_ref=dst,
            send_sem=tail_send.at[TAIL_SEND[n]],
            recv_sem=tail_recv.at[TAIL_RECV[n]],
            device_id=dev,
            device_id_type=MESH,
        )

    x0, x1, x2, x3 = ix, (ix + 1) % 4, (ix + 2) % 4, (ix + 3) % 4
    totals = (out_acc, gradx_acc)
    cores = {}
    for n, at in ((0, x2), (1, x1), (2, x3), (3, x0)):
        for arr in range(2):
            tail_out[at, arr] = totals[arr][at * 2 + other].astype(BF16)
        cores[n] = last(n, tail_out.at[at], tail_core.at[at], sibling)
        cores[n].start()

    def both(n, at):
        cores[n].wait_recv()
        for arr in range(2):
            mine = totals[arr][at * 2 + core] + tail_core[at, arr].astype(F32)
            tail[at, arr] = mine.astype(BF16)

    halves = (pl.ds(0, 16), pl.ds(16, 16))
    steps = (
        [last(4 + h, tail.at[x2, 0, rows], tail_h.at[0, rows], right) for h, rows in enumerate(halves)]
        + [last(6 + h, tail.at[x2, 1, rows], tail_h.at[1, rows], left) for h, rows in enumerate(halves)]
        + [
            last(8, tail.at[x1, 1], tail_f.at[0, 1], right),
            last(9, tail.at[x3, 0], tail_f.at[1, 0], left),
        ]
        + [last(10, tail.at[x1, 0, rows], tail_f.at[0, 0, rows], right) for rows in halves]
        + [last(11, tail.at[x3, 1, rows], tail_f.at[1, 1, rows], left) for rows in halves]
    )
    lax.fori_loop(0, 2, down_group, 0)
    both(0, x2)
    for n in range(4):
        steps[n].start()
    both(1, x1)
    steps[4].start()
    both(2, x3)
    steps[5].start()
    lax.fori_loop(2, 6, down_group, 0)
    lax.fori_loop(0, 2, gate_group, 0)
    for h, rows in enumerate(halves):
        steps[h].wait_recv()
        tail[x1, 0, rows] = plus(tail[x1, 0, rows], tail_h[0, rows])
        steps[6 + h].start()
        steps[2 + h].wait_recv()
        tail[x3, 1, rows] = plus(tail[x3, 1, rows], tail_h[1, rows])
        steps[8 + h].start()
    lax.fori_loop(2, 6, gate_group, 0)
    cores[3].wait_recv()
    last(8, tail_f, tail_f, right).wait_recv()
    for arr in range(2):
        total = totals[arr][x0 * 2 + core] + tail_core[x0, arr].astype(F32)
        total = total + tail_f[0, arr].astype(F32) + tail_f[1, arr].astype(F32)
        layer_ref[arr] = total.astype(BF16)

    most = terms.at[:, pl.ds(0, 3)]
    copy(0, 0, most, most, right).wait_send()
    copy(0, 6, terms.at[:, pl.ds(0, 3), 0], terms.at[:, pl.ds(0, 3), 0], right).wait_send()
    copy(0, 14, most, most, right).wait_send()
    last(0, tail_out, tail_core, sibling).wait_send()
    last(4, tail.at[pl.ds(0, 3)], tail.at[pl.ds(0, 3)], right).wait_send()
    head(0, xs.at[pl.ds(0, 7)], xs.at[pl.ds(0, 7)], right).wait_send()


def run_layer(gate_slots, gate_count, down_slots, down_count, inputs, grad_out, gate_blocks, up_blocks, down_blocks):
    anywhere = pl.BlockSpec(memory_space=pl.ANY)
    scalars = pl.BlockSpec(memory_space=pltpu.SMEM)
    vmem = pl.BlockSpec(memory_space=pltpu.VMEM)
    raw = pltpu.VMEM((NB + 1, BLOCK, BLOCK), BF16)
    part = (48, BLOCK)
    return pl.pallas_call(
        layer_kernel,
        out_shape=(
            pltpu.VMEM((2, 32, WIDTH), BF16),
            raw,
            raw,
            raw,
        ),
        in_specs=[scalars] * 4 + [anywhere] * 5,
        out_specs=(vmem,) * 4,
        scratch_shapes=[
            pltpu.VMEM((8, 2, 32, WIDTH), BF16),
            pltpu.VMEM((CHUNKS, WIDTH, CHUNK), BF16),
            pltpu.VMEM((CHUNKS, WIDTH, CHUNK), BF16),
            pltpu.VMEM((CHUNKS, CHUNK, WIDTH), BF16),
            pltpu.VMEM((CHUNKS, 4, 2, 4) + part, BF16),
            pltpu.VMEM((CHUNKS, 2, 4) + part, BF16),
            pltpu.VMEM((CHUNKS, 2, 2, 4) + part, BF16),
            pltpu.VMEM((CHUNKS, 4, 2) + part, BF16),
            pltpu.VMEM((CHUNKS, 2) + part, BF16),
            pltpu.VMEM((CHUNKS, 2, 2) + part, BF16),
            pltpu.VMEM((CHUNKS, 4, 4, 2) + part, BF16),
            pltpu.VMEM((FPB, BLOCK, TOKENS), BF16),
            pltpu.VMEM((FPB, TOKENS, 2 * BLOCK), BF16),
            pltpu.VMEM((DPB, BLOCK, TOKENS), BF16),
            pltpu.VMEM((DPB, TOKENS, BLOCK), BF16),
            pltpu.VMEM((8, 32, WIDTH), F32),
            pltpu.VMEM((8, 32, WIDTH), F32),
            pltpu.VMEM((4, 2, 32, WIDTH), BF16),
            pltpu.VMEM((4, 2, 32, WIDTH), BF16),
            pltpu.VMEM((4, 2, 32, WIDTH), BF16),
            pltpu.VMEM((2, 32, WIDTH), BF16),
            pltpu.VMEM((2, 2, 32, WIDTH), BF16),
            pltpu.VMEM((2, 8, 128), jnp.int32),
            pltpu.SMEM((2, 8, 128), jnp.int32),
            pltpu.SemaphoreType.DMA((6,)),
            pltpu.SemaphoreType.DMA((1,)),
            pltpu.SemaphoreType.DMA((9,)),
            pltpu.SemaphoreType.DMA((3,)),
            pltpu.SemaphoreType.DMA((CHUNKS, 8)),
            pltpu.SemaphoreType.DMA((2,)),
            pltpu.SemaphoreType.DMA((9,)),
        ],
        compiler_params=pltpu.CompilerParams(
            collective_id=0, has_side_effects=True, vmem_limit_bytes=51 * 2**20
        ),
        name="layer",
    )(gate_slots, gate_count, down_slots, down_count, inputs, grad_out, gate_blocks, up_blocks, down_blocks)


def save_kernel(
    layer, gate, up, down, out_ref, gradx_ref, gate_out, up_out, down_out, sem
):
    pairs = ((gate, gate_out), (up, up_out), (down, down_out))
    quarters = [pl.ds(q * (NB // 4), NB // 4) for q in range(4)]
    saves = [
        pltpu.make_async_copy(here.at[rows], out.at[rows], sem.at[n, q])
        for q, rows in enumerate(quarters)
        for n, (here, out) in enumerate(pairs)
    ]
    for save in saves:
        save.start()
    out_ref[...] = layer[0]
    gradx_ref[...] = layer[1]
    for save in saves:
        save.wait()


def run_save(layer, *grads):
    vmem = pl.BlockSpec(memory_space=pltpu.VMEM)
    anywhere = pl.BlockSpec(memory_space=pl.ANY)
    tokens = jax.ShapeDtypeStruct((32, WIDTH), BF16)
    blocks = jax.ShapeDtypeStruct((NB, BLOCK, BLOCK), BF16)
    return pl.pallas_call(
        save_kernel,
        out_shape=(tokens, tokens, blocks, blocks, blocks),
        in_specs=[vmem] + [anywhere] * 3,
        out_specs=(vmem, vmem, anywhere, anywhere, anywhere),
        scratch_shapes=[pltpu.SemaphoreType.DMA((3, 4))],
        compiler_params=pltpu.CompilerParams(vmem_limit_bytes=16 * 2**20),
        name="save",
    )(layer, *grads)


def local(
    inputs,
    grad_out,
    gate_blocks,
    up_blocks,
    down_blocks,
    gate_slots,
    gate_count,
    down_slots,
    down_count,
):
    layer, *grads = run_layer(
        gate_slots,
        gate_count,
        down_slots,
        down_count,
        inputs,
        grad_out,
        gate_blocks[0, 0],
        up_blocks[0, 0],
        down_blocks[0, 0],
    )
    layer_out, grad_x, *grads = run_save(layer, *grads)
    return (layer_out, grad_x) + tuple(grad[None, None] for grad in grads)


def solution(mesh):
    tokens = P("col", "row")
    blocks = P("row", "col", None, None, None)
    slots = P("row", "col", None)
    count = P("row", "col")
    return jax.shard_map(
        local,
        mesh=mesh,
        in_specs=(tokens, tokens, blocks, blocks, blocks, slots, count, slots, count),
        out_specs=(tokens, tokens, blocks, blocks, blocks),
        check_vma=False,
    )
```

```python
import jax
import jax.numpy as jnp
from jax import lax
from jax.experimental import pallas as pl
from jax.experimental.pallas import tpu as pltpu
from jax.sharding import PartitionSpec as P

TOKENS = 256
BLOCK = 128
NB = 96
DPB = 8
FPB = 26
WIDTH = DPB * BLOCK
CHUNK = 2 * BLOCK
CHUNKS = FPB // 2
GROUP = 16
LAGS = (0, 5, 10, 15, 20, 25, 30, 35, 40)
MESH = pl.DeviceIdType.MESH
TAIL_SEND = (0,) * 4 + (1,) * 8
TAIL_RECV = tuple(range(8)) + (8,) * 4
HEAD_SEM = (0, 1, 2, 3, 4, 5, 8, 8, 6, 7, 6, 7) + (8,) * 6
SEND_SEM = (0,) * 6 + (1,) * 8 + (2,) * 6
RECV_SEM = (0, 0, 1, 1, 1, 1, 2, 2, 3, 3, 4, 4, 5, 5, 6, 6, 7, 7, 7, 7)
F32 = jnp.float32
BF16 = jnp.bfloat16


def nt_dot(a, b):
    return lax.dot_general(a, b, (((1,), (1,)), ((), ())), preferred_element_type=F32)


def layer_kernel(
    gate_slots,
    gate_count,
    down_slots,
    down_count,
    x_in,
    cot_in,
    gate_in,
    up_in,
    down_in,
    layer_ref,
    raw_gate,
    raw_up,
    raw_down,
    xs,
    w_gate,
    w_up,
    w_down,
    terms,
    half_a,
    full_a,
    sums,
    half_b,
    full_b,
    acts,
    hidden_t,
    pairs,
    x_t,
    cots,
    out_acc,
    gradx_acc,
    tail_out,
    tail,
    tail_core,
    tail_h,
    tail_f,
    tables,
    slot_at,
    load_sem,
    head_send,
    head_recv,
    send_sem,
    recv_sem,
    tail_send,
    tail_recv,
):
    row, col = lax.axis_index("row"), lax.axis_index("col")
    z, y = row // 4, row % 4
    ix, core = col // 2, col % 2

    def y_dev(step):
        return (z * 4 + (y + step) % 4, col)

    def z_dev(step):
        return (((z + step) % 4) * 4 + y, col)

    def x_dev(step):
        return (row, ((ix + step) % 4) * 2 + core)

    sibling = (row, ix * 2 + 1 - core)

    loads = [
        pltpu.make_async_copy(x_in, xs.at[col, 0], load_sem.at[0]),
        pltpu.make_async_copy(cot_in, xs.at[col, 1], load_sem.at[1]),
        pltpu.make_async_copy(gate_in, raw_gate.at[pl.ds(0, NB)], load_sem.at[2]),
        pltpu.make_async_copy(up_in, raw_up.at[pl.ds(0, NB)], load_sem.at[3]),
        pltpu.make_async_copy(down_in, raw_down.at[pl.ds(0, NB)], load_sem.at[4]),
    ]
    loads[0].start()
    loads[1].start()

    barrier = pltpu.get_barrier_semaphore()
    for dev in (y_dev(1), y_dev(3), z_dev(1), z_dev(3), x_dev(1), x_dev(3), sibling):
        pl.semaphore_signal(barrier, inc=1, device_id=dev, device_id_type=MESH)

    zero = jnp.zeros((BLOCK, BLOCK), BF16)
    raw_gate[NB] = zero
    raw_up[NB] = zero
    raw_down[NB] = zero
    out_acc[...] = jnp.zeros_like(out_acc)
    gradx_acc[...] = jnp.zeros_like(gradx_acc)

    pl.semaphore_wait(barrier, 7)

    def head(n, src, dst, dev):
        return pltpu.make_async_remote_copy(
            src_ref=src,
            dst_ref=dst,
            send_sem=head_send.at[0],
            recv_sem=head_recv.at[HEAD_SEM[n]],
            device_id=dev,
            device_id_type=MESH,
        )

    other = 1 - core
    right, left = x_dev(1), x_dev(3)

    def at_x(step, side, arr, rows=pl.ds(0, 32)):
        return xs.at[((ix + step) % 4) * 2 + side, arr, rows]

    def head_start(n, src, dst, dev):
        head(n, src, dst, dev).start()

    def forward(n, ref, dev):
        head_start(n, ref, ref, dev)

    def head_wait(n, ref):
        head(n, ref, ref, right).wait_recv()

    first, second = pl.ds(0, 16), pl.ds(16, 16)
    head_start(0, x_in.at[first], xs.at[col, 0, first], right)
    head_start(1, cot_in.at[first], xs.at[col, 1, first], left)
    head_start(2, x_in.at[second], xs.at[col, 0, second], right)
    head_start(3, cot_in.at[second], xs.at[col, 1, second], left)
    head_start(4, cot_in, xs.at[col, 1], right)
    head_start(5, x_in, xs.at[col, 0], left)
    head_start(6, x_in, xs.at[col, 0], sibling)
    head_start(7, cot_in, xs.at[col, 1], sibling)
    for load in loads[2:]:
        load.start()

    spots = lax.broadcasted_iota(jnp.int32, (8, 128), 0) * 128 + lax.broadcasted_iota(
        jnp.int32, (8, 128), 1
    )

    def enter(n, both):
        gate_tab, down_tab = both
        gate_tab = jnp.where(spots == gate_slots[0, 0, n], n, gate_tab)
        down_tab = jnp.where(spots == down_slots[0, 0, n], n, down_tab)
        return gate_tab, down_tab

    nowhere = jnp.full((8, 128), NB, jnp.int32)
    gate_tab, down_tab = lax.fori_loop(0, NB, enter, (nowhere, nowhere), unroll=8)
    tables[0] = jnp.where(gate_tab < gate_count[0, 0], gate_tab, NB)
    tables[1] = jnp.where(down_tab < down_count[0, 0], down_tab, NB)
    to_scalars = pltpu.make_async_copy(tables, slot_at, load_sem.at[5])
    to_scalars.start()

    def find(table, spot):
        return slot_at[table, spot // 128, spot % 128]

    def place_gate(k, carry):
        for raw, dense in ((raw_gate, w_gate), (raw_up, w_up)):
            for r in range(DPB):
                for b in range(2):
                    slot = find(0, r * FPB + 2 * k + b)
                    dense[k, r * BLOCK : (r + 1) * BLOCK, b * BLOCK : (b + 1) * BLOCK] = raw[slot]
        return carry

    def place_down(k, carry):
        for r in range(DPB):
            for b in range(2):
                slot = find(1, r * FPB + 2 * k + b)
                w_down[k, b * BLOCK : (b + 1) * BLOCK, r * BLOCK : (r + 1) * BLOCK] = raw_down[slot]
        return carry

    to_scalars.wait()
    loads[2].wait()
    loads[3].wait()
    lax.fori_loop(0, 4, place_gate, 0)

    head_wait(0, at_x(3, core, 0, first))
    forward(8, at_x(3, core, 0, first), right)
    head_wait(1, at_x(1, core, 1, first))
    forward(9, at_x(1, core, 1, first), left)
    head_wait(2, at_x(3, core, 0, second))
    forward(10, at_x(3, core, 0, second), right)
    forward(12, at_x(3, core, 0), sibling)
    head_wait(3, at_x(1, core, 1, second))
    forward(11, at_x(1, core, 1, second), left)
    forward(13, at_x(1, core, 1), sibling)

    lax.fori_loop(4, 8, place_gate, 0)

    head_wait(4, at_x(3, core, 1))
    forward(14, at_x(3, core, 1), sibling)
    head_wait(5, at_x(1, core, 0))
    forward(15, at_x(1, core, 0), sibling)

    lax.fori_loop(8, CHUNKS, place_gate, 0)
    loads[4].wait()
    lax.fori_loop(0, 4, place_down, 0)

    head_wait(8, at_x(2, core, 0))
    forward(16, at_x(2, core, 0), sibling)
    head_wait(9, at_x(2, core, 1))
    forward(17, at_x(2, core, 1), sibling)

    lax.fori_loop(4, CHUNKS, place_down, 0)

    head_wait(6, xs.at[pl.ds(0, 4)])
    loads[0].wait()
    loads[1].wait()

    def lay_out_inputs():
        for r in range(DPB):
            cols = slice(r * BLOCK, (r + 1) * BLOCK)
            x_t[r] = xs[:, 0, :, cols].reshape(TOKENS, BLOCK).T
            cots[r] = xs[:, 1, :, cols].reshape(TOKENS, BLOCK)

    def places(k):
        odd = (k + core) % 2
        i = (1 - odd) * y + odd * z
        j = (1 - odd) * z + odd * y

        def dev(step, along_z):
            y_new = (y + (1 - along_z) * step) % 4
            z_new = (z + along_z * step) % 4
            return (z_new * 4 + y_new, col)

        return i, j, dev(1, odd), dev(3, odd), dev(1, 1 - odd), dev(3, 1 - odd)

    def copy(k, n, src, dst, dev):
        return pltpu.make_async_remote_copy(
            src_ref=src,
            dst_ref=dst,
            send_sem=send_sem.at[SEND_SEM[n]],
            recv_sem=recv_sem.at[k, RECV_SEM[n]],
            device_id=dev,
            device_id_type=MESH,
        )

    def all_copies(k):
        i, j, ar, al, br, bl = places(k)
        i1, i2, i3 = (i + 1) % 4, (i + 2) % 4, (i + 3) % 4
        j1, j2, j3 = (j + 1) % 4, (j + 2) % 4, (j + 3) % 4
        same = lambda n, ref, dev: copy(k, n, ref, ref, dev)
        near, rest = pl.ds(0, 2), pl.ds(2, 2)
        return [
            lambda: copy(k, 0, terms.at[k, i2, 0], half_a.at[k, 0], ar),
            lambda: copy(k, 1, terms.at[k, i2, 1], half_a.at[k, 1], al),
            lambda: copy(k, 2, terms.at[k, i1, 1], full_a.at[k, 0, 1], ar),
            lambda: copy(k, 3, terms.at[k, i3, 0], full_a.at[k, 1, 0], al),
            lambda: copy(k, 4, terms.at[k, i1, 0], full_a.at[k, 0, 0], ar),
            lambda: copy(k, 5, terms.at[k, i3, 1], full_a.at[k, 1, 1], al),
            lambda: copy(k, 6, sums.at[k, j2, 0], half_b.at[k, 0], br),
            lambda: copy(k, 7, sums.at[k, j2, 1], half_b.at[k, 1], bl),
            lambda: copy(k, 8, sums.at[k, j1], full_b.at[k, 0], br),
            lambda: copy(k, 9, sums.at[k, j3], full_b.at[k, 1], bl),
            lambda: same(10, acts.at[k, i, j], br),
            lambda: same(11, acts.at[k, i, j], bl),
            lambda: same(12, acts.at[k, i, j3, 0], br),
            lambda: same(13, acts.at[k, i, j1, 1], bl),
            lambda: same(14, acts.at[k, i, near], ar),
            lambda: same(15, acts.at[k, i, rest], al),
            lambda: same(16, acts.at[k, i, rest], ar),
            lambda: same(17, acts.at[k, i, near], al),
            lambda: same(18, acts.at[k, i3, near], ar),
            lambda: same(19, acts.at[k, i1, rest], al),
        ]

    def arrived(k, n, ref):
        i, j, ar, al, br, bl = places(k)
        copy(k, n, ref, ref, ar).wait_recv()

    def plus(a, b):
        return (a.astype(F32) + b.astype(F32)).astype(BF16)

    def p0(k):
        for part, (arr, weights) in enumerate(((0, w_gate), (0, w_up), (1, w_down))):
            if part < 2:
                lhs = xs[:, 0].reshape(TOKENS, WIDTH)
                val = jnp.dot(lhs, weights[k], preferred_element_type=F32)
            else:
                lhs = xs[:, 1].reshape(TOKENS, WIDTH)
                val = nt_dot(lhs, weights[k])
            val = val.astype(BF16)
            for b in range(2):
                terms[k, :, b, :, part * 16 : (part + 1) * 16, :] = val[
                    :, b * BLOCK : (b + 1) * BLOCK
                ].reshape(4, 4, 16, BLOCK)
        copies = all_copies(k)
        for n in range(4):
            copies[n]().start()

    def p1(k):
        i, j, *_ = places(k)
        i1, i3 = (i + 1) % 4, (i + 3) % 4
        copies = all_copies(k)
        arrived(k, 0, half_a.at[k])
        terms[k, i1, 0] = plus(terms[k, i1, 0], half_a[k, 0])
        copies[4]().start()
        terms[k, i3, 1] = plus(terms[k, i3, 1], half_a[k, 1])
        copies[5]().start()

    def p2(k):
        i, j, *_ = places(k)
        copies = all_copies(k)
        arrived(k, 2, full_a.at[k])
        for b in range(2):
            total = terms[k, i, b].astype(F32) + full_a[k, 0, b].astype(F32)
            sums[k, :, b] = (total + full_a[k, 1, b].astype(F32)).astype(BF16)
        copies[6]().start()
        copies[7]().start()

    def p3(k):
        i, j, *_ = places(k)
        j1, j3 = (j + 1) % 4, (j + 3) % 4
        copies = all_copies(k)
        arrived(k, 6, half_b.at[k])
        sums[k, j1, 0] = plus(sums[k, j1, 0], half_b[k, 0])
        copies[8]().start()
        sums[k, j3, 1] = plus(sums[k, j3, 1], half_b[k, 1])
        copies[9]().start()

    def p4(k):
        i, j, *_ = places(k)
        copies = all_copies(k)
        arrived(k, 8, full_b.at[k])
        total = sums[k, j].astype(F32) + full_b[k, 0].astype(F32) + full_b[k, 1].astype(F32)
        gate, up, grad = total[:, 0:16], total[:, 16:32], total[:, 32:48]
        sigma = 1.0 / (1.0 + jnp.exp(-gate))
        acts[k, i, j, :, 0:16, :] = (gate * sigma * up).astype(BF16)
        acts[k, i, j, :, 16:32, :] = (grad * up * sigma * (1.0 + gate * (1.0 - sigma))).astype(BF16)
        acts[k, i, j, :, 32:48, :] = (grad * gate * sigma).astype(BF16)
        copies[10]().start()
        copies[11]().start()

    def p5(k):
        i, j, *_ = places(k)
        copies = all_copies(k)
        arrived(k, 10, acts.at[k, i, pl.ds(0, 2)])
        copies[12]().start()
        copies[13]().start()

    def p6(k):
        i, j, *_ = places(k)
        copies = all_copies(k)
        arrived(k, 12, acts.at[k, i, 0])
        for n in range(14, 18):
            copies[n]().start()

    def p7(k):
        i, j, *_ = places(k)
        copies = all_copies(k)
        arrived(k, 14, acts.at[k, 0])
        copies[18]().start()
        copies[19]().start()

    def p8(k):
        i, j, *_ = places(k)
        arrived(k, 16, acts.at[k, pl.ds(0, 2)])

        def act(part):
            cols = [
                acts[k, :, :, b, part * 16 : (part + 1) * 16, :].reshape(TOKENS, BLOCK)
                for b in range(2)
            ]
            return cols, jnp.concatenate(cols, axis=1)

        (_, hidden), (gate_cols, grad_gate), (up_cols, grad_up) = act(0), act(1), act(2)
        for n in range(4):
            cols = slice(n * 256, (n + 1) * 256)
            out = jnp.dot(hidden, w_down[k, :, cols], preferred_element_type=F32)
            out_acc[:, :, cols] += out.reshape(8, 32, 256)
            grad = nt_dot(grad_gate, w_gate[k, cols, :]) + nt_dot(grad_up, w_up[k, cols, :])
            gradx_acc[:, :, cols] += grad.reshape(8, 32, 256)
        hidden_t[pl.ds(2 * k, 2)] = hidden.T.reshape(2, BLOCK, TOKENS)
        for b in range(2):
            pairs[2 * k + b, :, 0:BLOCK] = gate_cols[b]
            pairs[2 * k + b, :, BLOCK:] = up_cols[b]

    def tick(t, carry):
        for phase, late in zip((p7, p6, p5, p4, p3, p2, p1, p0, p8), LAGS[7::-1] + LAGS[8:]):
            k = t - late

            @pl.when(jnp.logical_and(k >= 0, k < CHUNKS))
            def _():
                phase(k)

        @pl.when(t == 6)
        def _():
            lay_out_inputs()

        return carry

    lax.fori_loop(0, CHUNKS + LAGS[8], tick, 0)

    def down_group(g, carry):
        for u in range(GROUP):
            n = g * GROUP + u
            spot = down_slots[0, 0, n]
            val = jnp.dot(hidden_t[spot % FPB], cots[spot // FPB], preferred_element_type=F32)
            raw_down[n] = jnp.where(n < down_count[0, 0], val, 0.0).astype(BF16)
        return carry

    def gate_group(g, carry):
        for u in range(GROUP):
            n = g * GROUP + u
            spot = gate_slots[0, 0, n]
            val = jnp.dot(x_t[spot // FPB], pairs[spot % FPB], preferred_element_type=F32)
            val = jnp.where(n < gate_count[0, 0], val, 0.0).astype(BF16)
            raw_gate[n] = val[:, 0:BLOCK]
            raw_up[n] = val[:, BLOCK:]
        return carry

    def last(n, src, dst, dev):
        return pltpu.make_async_remote_copy(
            src_ref=src,
            dst_ref=dst,
            send_sem=tail_send.at[TAIL_SEND[n]],
            recv_sem=tail_recv.at[TAIL_RECV[n]],
            device_id=dev,
            device_id_type=MESH,
        )

    x0, x1, x2, x3 = ix, (ix + 1) % 4, (ix + 2) % 4, (ix + 3) % 4
    totals = (out_acc, gradx_acc)
    cores = {}
    for n, at in ((0, x2), (1, x1), (2, x3), (3, x0)):
        for arr in range(2):
            tail_out[at, arr] = totals[arr][at * 2 + other].astype(BF16)
        cores[n] = last(n, tail_out.at[at], tail_core.at[at], sibling)
        cores[n].start()

    def both(n, at):
        cores[n].wait_recv()
        for arr in range(2):
            mine = totals[arr][at * 2 + core] + tail_core[at, arr].astype(F32)
            tail[at, arr] = mine.astype(BF16)

    halves = (pl.ds(0, 16), pl.ds(16, 16))
    steps = (
        [last(4 + h, tail.at[x2, 0, rows], tail_h.at[0, rows], right) for h, rows in enumerate(halves)]
        + [last(6 + h, tail.at[x2, 1, rows], tail_h.at[1, rows], left) for h, rows in enumerate(halves)]
        + [
            last(8, tail.at[x1, 1], tail_f.at[0, 1], right),
            last(9, tail.at[x3, 0], tail_f.at[1, 0], left),
        ]
        + [last(10, tail.at[x1, 0, rows], tail_f.at[0, 0, rows], right) for rows in halves]
        + [last(11, tail.at[x3, 1, rows], tail_f.at[1, 1, rows], left) for rows in halves]
    )
    lax.fori_loop(0, 2, down_group, 0)
    both(0, x2)
    for n in range(4):
        steps[n].start()
    both(1, x1)
    steps[4].start()
    both(2, x3)
    steps[5].start()
    lax.fori_loop(2, 6, down_group, 0)
    lax.fori_loop(0, 2, gate_group, 0)
    for h, rows in enumerate(halves):
        steps[h].wait_recv()
        tail[x1, 0, rows] = plus(tail[x1, 0, rows], tail_h[0, rows])
        steps[6 + h].start()
        steps[2 + h].wait_recv()
        tail[x3, 1, rows] = plus(tail[x3, 1, rows], tail_h[1, rows])
        steps[8 + h].start()
    lax.fori_loop(2, 6, gate_group, 0)
    cores[3].wait_recv()
    last(8, tail_f, tail_f, right).wait_recv()
    for arr in range(2):
        total = totals[arr][x0 * 2 + core] + tail_core[x0, arr].astype(F32)
        total = total + tail_f[0, arr].astype(F32) + tail_f[1, arr].astype(F32)
        layer_ref[arr] = total.astype(BF16)

    most = terms.at[:, pl.ds(0, 3)]
    copy(0, 0, most, most, right).wait_send()
    copy(0, 6, terms.at[:, pl.ds(0, 3), 0], terms.at[:, pl.ds(0, 3), 0], right).wait_send()
    copy(0, 14, most, most, right).wait_send()
    last(0, tail_out, tail_core, sibling).wait_send()
    last(4, tail.at[pl.ds(0, 3)], tail.at[pl.ds(0, 3)], right).wait_send()
    head(0, xs.at[pl.ds(0, 7)], xs.at[pl.ds(0, 7)], right).wait_send()


def run_layer(gate_slots, gate_count, down_slots, down_count, inputs, grad_out, gate_blocks, up_blocks, down_blocks):
    anywhere = pl.BlockSpec(memory_space=pl.ANY)
    scalars = pl.BlockSpec(memory_space=pltpu.SMEM)
    vmem = pl.BlockSpec(memory_space=pltpu.VMEM)
    raw = pltpu.VMEM((NB + 1, BLOCK, BLOCK), BF16)
    part = (48, BLOCK)
    return pl.pallas_call(
        layer_kernel,
        out_shape=(
            pltpu.VMEM((2, 32, WIDTH), BF16),
            raw,
            raw,
            raw,
        ),
        in_specs=[scalars] * 4 + [anywhere] * 5,
        out_specs=(vmem,) * 4,
        scratch_shapes=[
            pltpu.VMEM((8, 2, 32, WIDTH), BF16),
            pltpu.VMEM((CHUNKS, WIDTH, CHUNK), BF16),
            pltpu.VMEM((CHUNKS, WIDTH, CHUNK), BF16),
            pltpu.VMEM((CHUNKS, CHUNK, WIDTH), BF16),
            pltpu.VMEM((CHUNKS, 4, 2, 4) + part, BF16),
            pltpu.VMEM((CHUNKS, 2, 4) + part, BF16),
            pltpu.VMEM((CHUNKS, 2, 2, 4) + part, BF16),
            pltpu.VMEM((CHUNKS, 4, 2) + part, BF16),
            pltpu.VMEM((CHUNKS, 2) + part, BF16),
            pltpu.VMEM((CHUNKS, 2, 2) + part, BF16),
            pltpu.VMEM((CHUNKS, 4, 4, 2) + part, BF16),
            pltpu.VMEM((FPB, BLOCK, TOKENS), BF16),
            pltpu.VMEM((FPB, TOKENS, 2 * BLOCK), BF16),
            pltpu.VMEM((DPB, BLOCK, TOKENS), BF16),
            pltpu.VMEM((DPB, TOKENS, BLOCK), BF16),
            pltpu.VMEM((8, 32, WIDTH), F32),
            pltpu.VMEM((8, 32, WIDTH), F32),
            pltpu.VMEM((4, 2, 32, WIDTH), BF16),
            pltpu.VMEM((4, 2, 32, WIDTH), BF16),
            pltpu.VMEM((4, 2, 32, WIDTH), BF16),
            pltpu.VMEM((2, 32, WIDTH), BF16),
            pltpu.VMEM((2, 2, 32, WIDTH), BF16),
            pltpu.VMEM((2, 8, 128), jnp.int32),
            pltpu.SMEM((2, 8, 128), jnp.int32),
            pltpu.SemaphoreType.DMA((6,)),
            pltpu.SemaphoreType.DMA((1,)),
            pltpu.SemaphoreType.DMA((9,)),
            pltpu.SemaphoreType.DMA((3,)),
            pltpu.SemaphoreType.DMA((CHUNKS, 8)),
            pltpu.SemaphoreType.DMA((2,)),
            pltpu.SemaphoreType.DMA((9,)),
        ],
        compiler_params=pltpu.CompilerParams(
            collective_id=0, has_side_effects=True, vmem_limit_bytes=51 * 2**20
        ),
        name="layer",
    )(gate_slots, gate_count, down_slots, down_count, inputs, grad_out, gate_blocks, up_blocks, down_blocks)


def save_kernel(
    layer, gate, up, down, out_ref, gradx_ref, gate_out, up_out, down_out, sem
):
    pairs = ((gate, gate_out), (up, up_out), (down, down_out))
    quarters = [pl.ds(q * (NB // 4), NB // 4) for q in range(4)]
    saves = [
        pltpu.make_async_copy(here.at[rows], out.at[rows], sem.at[n, q])
        for q, rows in enumerate(quarters)
        for n, (here, out) in enumerate(pairs)
    ]
    for save in saves:
        save.start()
    out_ref[...] = layer[0]
    gradx_ref[...] = layer[1]
    for save in saves:
        save.wait()


def run_save(layer, *grads):
    vmem = pl.BlockSpec(memory_space=pltpu.VMEM)
    anywhere = pl.BlockSpec(memory_space=pl.ANY)
    tokens = jax.ShapeDtypeStruct((32, WIDTH), BF16)
    blocks = jax.ShapeDtypeStruct((NB, BLOCK, BLOCK), BF16)
    return pl.pallas_call(
        save_kernel,
        out_shape=(tokens, tokens, blocks, blocks, blocks),
        in_specs=[vmem] + [anywhere] * 3,
        out_specs=(vmem, vmem, anywhere, anywhere, anywhere),
        scratch_shapes=[pltpu.SemaphoreType.DMA((3, 4))],
        compiler_params=pltpu.CompilerParams(vmem_limit_bytes=16 * 2**20),
        name="save",
    )(layer, *grads)


def local(
    inputs,
    grad_out,
    gate_blocks,
    up_blocks,
    down_blocks,
    gate_slots,
    gate_count,
    down_slots,
    down_count,
):
    layer, *grads = run_layer(
        gate_slots,
        gate_count,
        down_slots,
        down_count,
        inputs,
        grad_out,
        gate_blocks[0, 0],
        up_blocks[0, 0],
        down_blocks[0, 0],
    )
    layer_out, grad_x, *grads = run_save(layer, *grads)
    return (layer_out, grad_x) + tuple(grad[None, None] for grad in grads)


def solution(mesh):
    tokens = P("col", "row")
    blocks = P("row", "col", None, None, None)
    slots = P("row", "col", None)
    count = P("row", "col")
    return jax.shard_map(
        local,
        mesh=mesh,
        in_specs=(tokens, tokens, blocks, blocks, blocks, slots, count, slots, count),
        out_specs=(tokens, tokens, blocks, blocks, blocks),
        check_vma=False,
    )
```
